32 devices in a mesh: tiles: 2 (over y), disp: 4 (over z), rows: 2 (over x), cols: 2 (over core).
Axes of the slice: x: 2, y: 2, z: 4, core: 2. Of those that a mesh axis runs over, the one named last changes fastest.
Arguments:
- left_feat: bfloat16 [4, 256, 320], P(('tiles', 'rows'), ('cols', 'disp')), parts along dimension 0, may hold values from -64 to 64
- right_feat: bfloat16 [4, 256, 320], P(('tiles', 'rows'), ('cols', 'disp')), parts along dimension 0, may hold values from -64 to 64
- conv_first: bfloat16 [27, 32, 40], replicated, may hold values from -0.1875 to 0.1875
- conv_mid: bfloat16 [2, 27, 32, 32], replicated, may hold values from -0.21875 to 0.21875
- conv_last: bfloat16 [27, 1, 32], replicated, may hold values from -3 to 3
Outputs:
- estimate: float32 [4, 256], P(('tiles', 'rows'), ('cols', 'disp')), parts along dimension 0
The draws below stay inside these ranges and needn't reach their ends.
There are 2 independent parts, one for each index of `tiles`. The reference program is written for one: setup_inputs(seed, part) draws one part's arguments, and reference() takes and returns one part's arrays. A program takes and returns all parts, laid end to end along the dimension named above; an argument that names none is the same for every part. Nothing has to cross between parts.
All inputs are finite; a program needn't handle non-finite values.
Results may differ from the reference program's by a relative error of at most 0.012.
The reference program's roundings to bfloat16 on the way (of `volume`) count: a program that leaves them out, or rounds other values in their place, can miss the bound.
Values may be sent and summed in bfloat16 or wider, within the bound.
No kernel may reach another device: no remote copies, remote signals or barrier semaphores. Data moves between devices by JAX's collectives and lax.ppermute only.
A program may use at most 64 MiB of HBM per device.

```python
import jax
import jax.numpy as jnp
from jax import lax

C = 320
G = 40
F = 32
MID = 2
DISP = 64
H = 2
W = 256


def boost_rows(key):
    base = jax.random.fold_in(key, 7)
    pick_key, mask_key, level_key = jax.random.split(base, 3)
    pick = jax.random.randint(pick_key, (), 0, H)
    chosen = (jax.random.randint(mask_key, (H,), 0, 8) == 0) | (jnp.arange(H) == pick)
    levels = jnp.array([7.0, 9.0, 11.0], jnp.float32)[jax.random.randint(level_key, (H,), 0, 3)]
    return jnp.where(chosen, levels, 1.0).astype(jnp.float32)[:, None, None]


def draw_features(key, salt):
    boost = boost_rows(key)
    own_key = jax.random.fold_in(key, salt)
    first_key = jax.random.fold_in(own_key, 0)
    values = jnp.clip(jax.random.normal(first_key, (H, W, C), jnp.float32), -4.0, 4.0)
    values = values * boost
    return values.astype(jnp.bfloat16)


def draw_left_feat(key, part):
    return draw_features(key, 11)


def draw_right_feat(key, part):
    return draw_features(key, 12)


def noise(key, extent, deviation, limit, held_as=jnp.bfloat16):
    result = deviation * jax.random.normal(key, extent, jnp.float32)
    return jnp.clip(result, min=-limit, max=limit).astype(held_as)


def setup_inputs(seed: int = 0, part: int = 0) -> dict:
    streams_of = jax.random.split(jax.random.key(seed), 6)
    part_splits = jax.random.split(jax.random.fold_in(streams_of[5], part), 6)
    return {
        "left_feat": draw_left_feat(jax.random.fold_in(jax.random.fold_in(streams_of[5], part), 71), part),
        "right_feat": draw_right_feat(jax.random.fold_in(jax.random.fold_in(streams_of[5], part), 71), part),
        "conv_first": noise(streams_of[2], (27, F, G), (27 * G) ** -0.5, 0.1875),
        "conv_mid": noise(streams_of[3], (MID, 27, F, F), (27 * F) ** -0.5, 0.21875),
        "conv_last": noise(streams_of[4], (27, 1, F), 0.5, 3.0),
    }


def conv_layer(inputs, kernel):
    taps = jnp.transpose(kernel, (1, 2, 0)).reshape(kernel.shape[1], kernel.shape[2], 3, 3, 3).astype(jnp.float32)
    planes = jnp.transpose(inputs, (1, 0, 2, 3))[None].astype(jnp.float32)
    output = lax.conv_general_dilated(planes, taps, (1, 1, 1), ((1, 1), (1, 1), (1, 1)), dimension_numbers=("NCDHW", "OIDHW", "NCDHW"), precision=lax.Precision.HIGHEST)
    return jnp.transpose(output[0], (1, 0, 2, 3))


def reference(left_feat, right_feat, conv_first, conv_mid, conv_last):
    group_size = C // G
    padded_right = jnp.pad(right_feat, ((0, 0), (DISP, 0), (0, 0)))
    left_groups = left_feat.astype(jnp.float32).reshape(H, W, G, group_size)

    def single(disp_value):
        shifted = lax.dynamic_slice_in_dim(padded_right, (DISP - disp_value).astype(jnp.int32), W, 1)
        right_groups = shifted.astype(jnp.float32).reshape(H, W, G, group_size)
        corr = jnp.sum(left_groups * right_groups, axis=3) / group_size
        return jnp.transpose(corr, (2, 0, 1)).astype(jnp.bfloat16)

    volume = lax.map(single, jnp.arange(DISP, dtype=jnp.int32))
    hidden = jax.nn.relu(conv_layer(volume, conv_first))
    for layer in range(MID):
        hidden = jax.nn.relu(conv_layer(hidden, conv_mid[layer]))
    cost_cube = conv_layer(hidden, conv_last)[:, 0]
    highest = jnp.max(cost_cube, axis=0)
    weights = jnp.exp(cost_cube - highest[None])
    levels = (jnp.arange(DISP, dtype=jnp.float32) / DISP)[:, None, None]
    return jnp.sum(weights * levels, axis=0) / jnp.sum(weights, axis=0)
```

```python
import jax
import jax.numpy as jnp
from jax import lax
from jax.experimental import pallas as pl
from jax.experimental.pallas import tpu as pltpu
from jax.sharding import PartitionSpec as P

MID = 2
DDEV = 16


def extended_2(block, sides, width):
    for axis, dim in sides:
        count = lax.axis_size(axis)
        forward = [(i, i + 1) for i in range(count - 1)]
        backward = [(target, source) for source, target in forward]
        low = lax.ppermute(
            lax.slice_in_dim(block, block.shape[dim] - width, None, axis=dim), axis, forward
        )
        high = lax.ppermute(lax.slice_in_dim(block, 0, width, axis=dim), axis, backward)
        block = jnp.concatenate([low, block, high], axis=dim)
    return block


def passed_along(x, axis, by):
    peers = lax.axis_size(axis)
    pairs = [(i, i + by) for i in range(peers) if 0 <= i + by < peers]
    return lax.ppermute(x, axis, pairs)


def combined_all(part, axis, combine):
    gathered = jax.tree.map(lambda a: lax.all_gather(a, axis), part)

    def take(source):
        return jax.tree.map(lambda a: lax.dynamic_index_in_dim(a, source, 0, False), gathered)

    return lax.fori_loop(
        1, lax.axis_size(axis), lambda source, state: combine(state, take(source)), take(0)
    )


def correlate(left_full, extended, groups, first_disp, count, total_disp):
    rows_here, width_here, channels = left_full.shape
    group_size = channels // groups
    left_groups = left_full.reshape(rows_here, width_here, groups, group_size)

    def single(offset):
        disp_value = first_disp + offset
        shifted = lax.dynamic_slice_in_dim(extended, 2 * width_here - disp_value, width_here, 1)
        right_groups = shifted.reshape(rows_here, width_here, groups, group_size)
        corr = (
            jnp.einsum(
                "hwgc,hwgc->ghw", left_groups, right_groups, preferred_element_type=jnp.float32
            )
            / group_size
        )
        inside = (disp_value >= 0) & (disp_value < total_disp)
        return jnp.where(inside, corr, 0.0).astype(jnp.bfloat16)

    return lax.map(single, jnp.arange(count, dtype=jnp.int32))


def convolve(padded, kernel):
    depth_out = padded.shape[0] - 2
    in_chans = padded.shape[1]
    rows_out = padded.shape[2] - 2
    cols_out = padded.shape[3] - 2
    out_chans = kernel.shape[1]
    columns = jnp.concatenate(
        [
            padded[:, :, row_tap : row_tap + rows_out, col_tap : col_tap + cols_out]
            for row_tap in range(3)
            for col_tap in range(3)
        ],
        axis=1,
    )
    flat = columns.reshape(depth_out + 2, 9 * in_chans, rows_out * cols_out)
    summed = jnp.zeros((depth_out, out_chans, rows_out * cols_out), jnp.float32)
    for disp_tap in range(3):
        taps = (
            jnp.transpose(kernel[9 * disp_tap : 9 * disp_tap + 9], (1, 0, 2))
            .reshape(out_chans, 9 * in_chans)
            .astype(flat.dtype)
        )
        summed = summed + jnp.einsum(
            "ok,dkn->don",
            taps,
            flat[disp_tap : disp_tap + depth_out],
            preferred_element_type=jnp.float32,
            precision=lax.Precision.HIGHEST,
        )
    return summed.reshape(depth_out, out_chans, rows_out, cols_out)


def widen(hidden):
    return extended_2(hidden, (("disp", 0), ("rows", 2), ("cols", 3)), 1)


def combine_parts(earlier, later):
    highest = jnp.maximum(earlier[0], later[0])
    scale_one = jnp.exp(earlier[0] - highest)
    scale_two = jnp.exp(later[0] - highest)
    return (
        highest,
        earlier[1] * scale_one + later[1] * scale_two,
        earlier[2] * scale_one + later[2] * scale_two,
    )


def general(left_feat, right_feat, conv_first, conv_mid, conv_last):
    piece_width = left_feat.shape[1]
    groups = conv_first.shape[2]
    disp_count = lax.axis_size("disp")
    depth_here = DDEV
    total_disp = depth_here * disp_count
    first_disp = lax.axis_index("disp") * depth_here
    left_full, right_full = (
        lax.all_gather(left_feat, "disp", axis=1, tiled=True),
        lax.all_gather(right_feat, "disp", axis=1, tiled=True),
    )
    prior_full = passed_along(right_full, "cols", 1)
    extended = jnp.concatenate([jnp.zeros_like(right_full), prior_full, right_full], axis=1)
    volume = correlate(left_full, extended, groups, first_disp, depth_here, total_disp)
    padded = extended_2(volume, (("disp", 0), ("rows", 2), ("cols", 3)), 1)
    hidden = jax.nn.relu(convolve(padded, conv_first))
    for layer in range(MID):
        hidden = jax.nn.relu(convolve(widen(hidden), conv_mid[layer]))
    cost_cube = convolve(widen(hidden), conv_last)[:, 0]
    levels = (
        (first_disp + jnp.arange(depth_here, dtype=jnp.int32)).astype(jnp.float32) / total_disp
    )[:, None, None]
    local_high = jnp.max(cost_cube, axis=0)
    weights = jnp.exp(cost_cube - local_high[None])
    merged = combined_all(
        (local_high, jnp.sum(weights, axis=0), jnp.sum(weights * levels, axis=0)),
        "disp",
        combine_parts,
    )
    whole_row = merged[2] / merged[1]
    return lax.dynamic_slice_in_dim(whole_row, lax.axis_index("disp") * piece_width, piece_width, 1)


BF, F32 = jnp.bfloat16, jnp.float32
NT = (((1,), (1,)), ((), ()))


def dot(a, b, dims=(((1,), (0,)), ((), ()))):
    return lax.dot_general(a, b, dims, preferred_element_type=F32)


def iota(shape, dim):
    return lax.broadcasted_iota(jnp.int32, shape, dim)


def prep_kernel(cf_ref, cm_ref, cl_ref, w1_ref, wm_ref, wl_ref, perm_ref):
    own = lax.axis_index("rows")

    def strip(tap_of, a, h_in, eye):
        rows = []
        for e in (1, 0, -1):
            for h_out in (0, 1):
                rows.append(tap_of(9 * a + 3 * (h_in - h_out + 1) + (e + 1)))
        rows.append(jnp.zeros((64, rows[0].shape[1]), BF))
        return dot(eye, jnp.concatenate(rows, axis=0), NT)

    def placed(base, w_in):
        shift = 64 * (w_in - 1)
        lane = iota(base.shape, 1)
        moved = base if shift == 0 else pltpu.roll(base, shift % 256, axis=1)
        keep = (lane >= shift) & (lane < shift + 192)
        return jnp.where(keep, moved, 0.0).astype(BF)

    def eye_of(n):
        return (iota((n, n), 0) == iota((n, n), 1)).astype(F32).astype(BF)

    eye40, eye32 = eye_of(40), eye_of(32)
    for a in range(3):
        parts = [strip(lambda t: cf_ref[t], a, h_in, eye40) for h_in in (0, 1)]
        main = jnp.concatenate([p[:32] for p in parts], axis=0)
        rest = jnp.concatenate([p[32:] for p in parts], axis=0)
        w1_ref[a, 464:496] = jnp.zeros((32, 256), BF)
        for w_in in range(-1, 5):
            row = {-1: 320, 4: 256}.get(w_in, 64 * w_in)
            w1_ref[a, row : row + 64] = placed(main, w_in)
            row = {-1: 496, 4: 448}.get(w_in, 384 + 16 * w_in)
            w1_ref[a, row : row + 16] = placed(rest, w_in)
    for layer in range(2):
        for a in range(3):
            main = jnp.concatenate(
                [strip(lambda t: cm_ref[layer, t], a, h_in, eye32) for h_in in (0, 1)], axis=0
            )
            for w_in in range(-1, 5):
                block = placed(main, w_in)
                if w_in == 4:
                    rows = (256, 384)
                elif w_in == -1:
                    rows = (320, 448)
                else:
                    rows = (64 * w_in, 512 + 64 * w_in)
                for row in rows:
                    wm_ref[layer, a, row : row + 64] = block
    cl = cl_ref[...]
    clt = dot(eye32, cl, NT).astype(BF)
    for w_in in range(-1, 5):
        for h_in in (0, 1):
            lane = iota((27, 128), 1)
            a, e = lane // 4, w_in - lane % 4
            b = h_in - own
            tap = 9 * a + 3 * (b + 1) + (e + 1)
            ok = (a < 3) & (e >= -1) & (e <= 1) & (b >= -1) & (b <= 1)
            pick = (ok & (iota((27, 128), 0) == tap)).astype(F32).astype(BF)
            block = dot(clt, pick).astype(BF)
            if w_in == 4:
                rows = (256, 384)
            elif w_in == -1:
                rows = (320, 448)
            else:
                rows = (64 * w_in, 512 + 64 * w_in)
            for row in rows:
                wl_ref[row + 32 * h_in : row + 32 * h_in + 32] = block
    lane = iota((1, 1024), 1)
    src = ((lane // 32) % 2) * 384 + (lane % 32) * 8 + lane // 128
    perm_ref[:, :1024] = (iota((768, 1024), 0) == src).astype(F32).astype(BF)
    lane = iota((1, 512), 1)
    src = ((lane // 8) % 2) * 384 + (32 + lane % 8) * 8 + (lane // 128) * 2 + (lane // 64) % 2
    perm_ref[:, 1024:] = (iota((768, 512), 0) == src).astype(F32).astype(BF)


def prep(cf, cm, cl):
    vm = pl.BlockSpec(memory_space=pltpu.VMEM)
    return pl.pallas_call(
        prep_kernel,
        out_shape=(
            jax.ShapeDtypeStruct((3, 512, 256), BF),
            jax.ShapeDtypeStruct((2, 3, 768, 256), BF),
            jax.ShapeDtypeStruct((768, 128), BF),
            jax.ShapeDtypeStruct((768, 1536), BF),
        ),
        in_specs=[vm] * 3,
        out_specs=[vm] * 4,
        compiler_params=pltpu.CompilerParams(vmem_limit_bytes=40 * 2**20),
        name="prep",
    )(cf, cm, cl)


def main_body(load_r, load_l, w1_ref, wm_ref, wl_ref, perm_ref, out_ref, win, rs, lp, xb1, xb, ys):
    z = lax.axis_index("disp")
    core = lax.axis_index("cols")
    piece = core * 4 + z
    win[...] = jnp.zeros_like(win)

    def put(row, pair):
        for h in (0, 1):
            win[row : row + pair[h].shape[0], 384 * h : 384 * h + 320] = pair[h]

    put(0, load_r(1, 0, 16))
    put(16, load_r(-3, 16, 32))
    put(32, load_r(-2, 0, 32))
    put(64, load_r(-1, 0, 32))
    put(96, load_r(0, 0, 32))
    put(128, load_l(-1, 16, 32))
    put(144, load_l(0, 0, 32))
    put(176, load_l(1, 0, 16))
    zp = dot(win[...], perm_ref[...])
    for tile in range(12):
        lp[tile] = zp[128:, 128 * tile : 128 * tile + 128]
    zpr = zp[:128]
    lane = iota((128, 1024), 1)
    zm = jnp.concatenate(
        [jnp.where((lane // 64) % 2 == ww, zpr[:, :1024], 0.0).astype(BF) for ww in (0, 1)], axis=0
    )
    lane = iota((128, 512), 1)
    ze = jnp.concatenate(
        [jnp.where((lane // 16) % 4 == ww, zpr[:, 1024:], 0.0).astype(BF) for ww in range(4)], axis=0
    )
    s, q = iota((112, 512), 0), iota((112, 512), 1)
    r = q % 128
    rel = jnp.where(r < 16, 32 + r, r - 96)
    pick = (s == 40 + q // 128 - rel).astype(F32).astype(BF)
    rsm = dot(pick[:, :256], zm)
    rse = dot(pick, ze)
    for tile in range(8):
        rs[tile] = rsm[:, 128 * tile : 128 * tile + 128]
    for tile in range(4):
        rs[8 + tile] = rse[:, 128 * tile : 128 * tile + 128]

    lane1 = iota((1, 128), 1)
    low = lane1 < 64
    zero64 = jnp.zeros((64, 64), BF)
    xb1[0:64, 320:384] = zero64
    xb1[576:640, 256:320] = zero64
    kept = jnp.zeros((64, 128), BF)
    for wb in range(10):
        rows = slice(64 * wb, 64 * wb + 64)
        r0 = 12 + 4 * wb
        tiles = []
        for half in range(2):
            acc = None
            start = 44 - 4 * wb - 2 * half
            for c in range(8):
                left = jnp.where(
                    low,
                    lp[c, r0 + 2 * half : r0 + 2 * half + 1],
                    lp[c, r0 + 2 * half + 1 : r0 + 2 * half + 2],
                )
                term = left * rs[c, start : start + 64]
                acc = term if acc is None else acc + term
            tiles.append((acc * 0.125).astype(BF))
        acc = None
        start = 44 - 4 * wb
        group = (lane1 // 16) % 4
        for c in range(4):
            left = lp[8 + c, r0 : r0 + 1]
            for ww in (1, 2, 3):
                left = jnp.where(group == ww, lp[8 + c, r0 + ww : r0 + ww + 1], left)
            term = left * rs[8 + c, start : start + 64]
            acc = term if acc is None else acc + term
        rest = ((acc + pltpu.roll(acc, 64, axis=1)) * 0.125).astype(BF)
        xb1[rows, 0:128] = tiles[0]
        xb1[rows, 128:256] = tiles[1]
        xb1[rows, 384:512] = rest
        if wb > 0:
            before = slice(64 * wb - 64, 64 * wb)
            xb1[before, 256:320] = tiles[0][:, :64]
            xb1[before, 448:464] = rest[:, 64:80]
        xb1[rows, 496:512] = kept[:, 112:]
        if wb < 9:
            xb1[64 * wb + 64 : 64 * wb + 128, 320:384] = tiles[1][:, 64:]
        kept = rest
    xb1[576:640, 448:464] = jnp.zeros((64, 16), BF)

    first_ok = piece > 0
    last_ok = piece < 4 * lax.axis_size("cols") - 1
    ys[...] = jnp.zeros_like(ys)

    def layer(x, weights):
        ym = dot(x, weights(0))
        yc = dot(x, weights(1))
        yp = dot(x, weights(2))
        for tile in range(2):
            for wb in range(10):
                ys[tile, 0, wb, 8:72] = ym[64 * wb : 64 * wb + 64, 128 * tile : 128 * tile + 128]
                ys[tile, 1, wb, 8:72] = yp[64 * wb : 64 * wb + 64, 128 * tile : 128 * tile + 128]
        for wb in range(10):
            halves = []
            for tile in range(2):
                total = (
                    yc[64 * wb : 64 * wb + 64, 128 * tile : 128 * tile + 128]
                    + ys[tile, 0, wb, 7:71]
                    + ys[tile, 1, wb, 9:73]
                )
                total = jnp.maximum(total, 0.0)
                if wb == 0:
                    total = jnp.where(first_ok, total, 0.0)
                if wb == 9:
                    total = jnp.where(last_ok, total, 0.0)
                halves.append(total)
            rows = slice(64 * wb, 64 * wb + 64)
            for tile in range(2):
                hi = halves[tile].astype(BF)
                lo = (halves[tile] - hi.astype(F32)).astype(BF)
                for value, main, halo in ((hi, 0, 256), (lo, 512, 384)):
                    xb[rows, main + 128 * tile : main + 128 * tile + 128] = value
                    if tile == 0 and wb > 0:
                        xb[64 * wb - 64 : 64 * wb, halo : halo + 64] = value[:, :64]
                    if tile == 1 and wb < 9:
                        xb[64 * wb + 64 : 64 * wb + 128, halo + 64 : halo + 128] = value[:, 64:]

    for halo in (256, 384):
        xb[0:64, halo + 64 : halo + 128] = zero64
        xb[576:640, halo : halo + 64] = zero64
    layer(xb1[...], lambda a: w1_ref[a])
    layer(xb[...], lambda a: wm_ref[0, a])
    layer(xb[...], lambda a: wm_ref[1, a])
    y = dot(xb[64:576], wl_ref[...])
    for wb in range(8):
        ys[0, 0, wb, 8:72] = y[64 * wb : 64 * wb + 64]
    cost = jnp.zeros((64, 128), F32)
    for wb in range(8):
        part = None
        for a in range(3):
            term = ys[0, 0, wb, 7 + a : 71 + a]
            by = (4 * wb - 4 * a) % 128
            term = term if by == 0 else pltpu.roll(term, by, axis=1)
            part = term if part is None else part + term
        cost = jnp.where(lane1 // 4 == wb, part, cost)
    top = jnp.max(cost, axis=0, keepdims=True)
    weight = jnp.exp(cost - top)
    level = iota((64, 128), 0).astype(F32) * (1.0 / 64)
    est = jnp.sum(weight * level, axis=0, keepdims=True) / jnp.sum(weight, axis=0, keepdims=True)
    out_ref[...] = est[:, :32]


SCRATCH = [
    pltpu.VMEM((192, 768), BF),
    pltpu.VMEM((12, 112, 128), F32),
    pltpu.VMEM((12, 64, 128), F32),
    pltpu.VMEM((640, 512), BF),
    pltpu.VMEM((640, 768), BF),
    pltpu.VMEM((2, 2, 10, 80, 128), F32),
]


def main_kernel(*refs):
    g = refs[:8]
    w1, wm, wl, perm, out, win, rs, lp, xb1, xb, ys, stack = refs[8:]
    z, x, core = (lax.axis_index(n) for n in ("disp", "rows", "cols"))
    piece = core * 4 + z
    for i in range(8):
        stack[i] = g[i][...]

    def load(dp, base, lo, hi):
        want = piece + dp
        ok = (want >= 0) & (want < 8)
        want = jnp.clip(want, 0, 7)
        slot = 2 * (z ^ (want % 4)) + (core ^ (want // 4))
        return [
            jnp.where(ok, stack[slot, h ^ x, base + lo : base + hi], jnp.zeros((), BF)) for h in (0, 1)
        ]

    main_body(
        lambda dp, lo, hi: load(dp, 0, lo, hi),
        lambda dp, lo, hi: load(dp, 32, lo, hi),
        w1, wm, wl, perm, out, win, rs, lp, xb1, xb, ys,
    )


def fast(left_feat, right_feat, conv_first, conv_mid, conv_last):
    s = jnp.concatenate([right_feat, left_feat], axis=1)
    swap = [(0, 1), (1, 0)]
    s = jnp.concatenate([s, lax.ppermute(s, "rows", swap)], axis=0)
    a = [s] + [lax.ppermute(s, "disp", [(i, i ^ k) for i in range(4)]) for k in (1, 2, 3)]
    g = []
    for t in a:
        g += [t, lax.ppermute(t, "cols", swap)]
    ws = prep(conv_first, conv_mid, conv_last.reshape(27, 32))
    vm = pl.BlockSpec(memory_space=pltpu.VMEM)
    return pl.pallas_call(
        main_kernel,
        out_shape=jax.ShapeDtypeStruct((1, 32), F32),
        in_specs=[vm] * 12,
        out_specs=vm,
        scratch_shapes=SCRATCH + [pltpu.VMEM((8, 2, 64, 320), BF)],
        compiler_params=pltpu.CompilerParams(vmem_limit_bytes=48 * 2**20),
        name="cost_volume",
    )(*g, *ws)


def shards(left_feat, right_feat, conv_first, conv_mid, conv_last):
    sizes = tuple(lax.axis_size(name) for name in ("disp", "rows", "cols"))
    if sizes == (4, 2, 2) and left_feat.shape == (1, 32, 320) and conv_first.shape == (27, 32, 40):
        return fast(left_feat, right_feat, conv_first, conv_mid, conv_last)
    return general(left_feat, right_feat, conv_first, conv_mid, conv_last)


def solution(mesh):
    return jax.shard_map(
        shards,
        mesh=mesh,
        in_specs=(
            P(("tiles", "rows"), ("cols", "disp"), None),
            P(("tiles", "rows"), ("cols", "disp"), None),
            P(),
            P(),
            P(),
        ),
        out_specs=P(("tiles", "rows"), ("cols", "disp")),
        check_vma=False,
    )
```

```python
import jax
import jax.numpy as jnp
from jax import lax
from jax.experimental import pallas as pl
from jax.experimental.pallas import tpu as pltpu
from jax.sharding import PartitionSpec as P

MID = 2
DDEV = 16


def extended_2(block, sides, width):
    for axis, dim in sides:
        count = lax.axis_size(axis)
        forward = [(i, i + 1) for i in range(count - 1)]
        backward = [(target, source) for source, target in forward]
        low = lax.ppermute(
            lax.slice_in_dim(block, block.shape[dim] - width, None, axis=dim), axis, forward
        )
        high = lax.ppermute(lax.slice_in_dim(block, 0, width, axis=dim), axis, backward)
        block = jnp.concatenate([low, block, high], axis=dim)
    return block


def passed_along(x, axis, by):
    peers = lax.axis_size(axis)
    pairs = [(i, i + by) for i in range(peers) if 0 <= i + by < peers]
    return lax.ppermute(x, axis, pairs)


def combined_all(part, axis, combine):
    gathered = jax.tree.map(lambda a: lax.all_gather(a, axis), part)

    def take(source):
        return jax.tree.map(lambda a: lax.dynamic_index_in_dim(a, source, 0, False), gathered)

    return lax.fori_loop(
        1, lax.axis_size(axis), lambda source, state: combine(state, take(source)), take(0)
    )


def correlate(left_full, extended, groups, first_disp, count, total_disp):
    rows_here, width_here, channels = left_full.shape
    group_size = channels // groups
    left_groups = left_full.reshape(rows_here, width_here, groups, group_size)

    def single(offset):
        disp_value = first_disp + offset
        shifted = lax.dynamic_slice_in_dim(extended, 2 * width_here - disp_value, width_here, 1)
        right_groups = shifted.reshape(rows_here, width_here, groups, group_size)
        corr = (
            jnp.einsum(
                "hwgc,hwgc->ghw", left_groups, right_groups, preferred_element_type=jnp.float32
            )
            / group_size
        )
        inside = (disp_value >= 0) & (disp_value < total_disp)
        return jnp.where(inside, corr, 0.0).astype(jnp.bfloat16)

    return lax.map(single, jnp.arange(count, dtype=jnp.int32))


def convolve(padded, kernel):
    depth_out = padded.shape[0] - 2
    in_chans = padded.shape[1]
    rows_out = padded.shape[2] - 2
    cols_out = padded.shape[3] - 2
    out_chans = kernel.shape[1]
    columns = jnp.concatenate(
        [
            padded[:, :, row_tap : row_tap + rows_out, col_tap : col_tap + cols_out]
            for row_tap in range(3)
            for col_tap in range(3)
        ],
        axis=1,
    )
    flat = columns.reshape(depth_out + 2, 9 * in_chans, rows_out * cols_out)
    summed = jnp.zeros((depth_out, out_chans, rows_out * cols_out), jnp.float32)
    for disp_tap in range(3):
        taps = (
            jnp.transpose(kernel[9 * disp_tap : 9 * disp_tap + 9], (1, 0, 2))
            .reshape(out_chans, 9 * in_chans)
            .astype(flat.dtype)
        )
        summed = summed + jnp.einsum(
            "ok,dkn->don",
            taps,
            flat[disp_tap : disp_tap + depth_out],
            preferred_element_type=jnp.float32,
            precision=lax.Precision.HIGHEST,
        )
    return summed.reshape(depth_out, out_chans, rows_out, cols_out)


def widen(hidden):
    return extended_2(hidden, (("disp", 0), ("rows", 2), ("cols", 3)), 1)


def combine_parts(earlier, later):
    highest = jnp.maximum(earlier[0], later[0])
    scale_one = jnp.exp(earlier[0] - highest)
    scale_two = jnp.exp(later[0] - highest)
    return (
        highest,
        earlier[1] * scale_one + later[1] * scale_two,
        earlier[2] * scale_one + later[2] * scale_two,
    )


def general(left_feat, right_feat, conv_first, conv_mid, conv_last):
    piece_width = left_feat.shape[1]
    groups = conv_first.shape[2]
    disp_count = lax.axis_size("disp")
    depth_here = DDEV
    total_disp = depth_here * disp_count
    first_disp = lax.axis_index("disp") * depth_here
    left_full, right_full = (
        lax.all_gather(left_feat, "disp", axis=1, tiled=True),
        lax.all_gather(right_feat, "disp", axis=1, tiled=True),
    )
    prior_full = passed_along(right_full, "cols", 1)
    extended = jnp.concatenate([jnp.zeros_like(right_full), prior_full, right_full], axis=1)
    volume = correlate(left_full, extended, groups, first_disp, depth_here, total_disp)
    padded = extended_2(volume, (("disp", 0), ("rows", 2), ("cols", 3)), 1)
    hidden = jax.nn.relu(convolve(padded, conv_first))
    for layer in range(MID):
        hidden = jax.nn.relu(convolve(widen(hidden), conv_mid[layer]))
    cost_cube = convolve(widen(hidden), conv_last)[:, 0]
    levels = (
        (first_disp + jnp.arange(depth_here, dtype=jnp.int32)).astype(jnp.float32) / total_disp
    )[:, None, None]
    local_high = jnp.max(cost_cube, axis=0)
    weights = jnp.exp(cost_cube - local_high[None])
    merged = combined_all(
        (local_high, jnp.sum(weights, axis=0), jnp.sum(weights * levels, axis=0)),
        "disp",
        combine_parts,
    )
    whole_row = merged[2] / merged[1]
    return lax.dynamic_slice_in_dim(whole_row, lax.axis_index("disp") * piece_width, piece_width, 1)


BF, F32 = jnp.bfloat16, jnp.float32
NT = (((1,), (1,)), ((), ()))


def dot(a, b, dims=(((1,), (0,)), ((), ()))):
    return lax.dot_general(a, b, dims, preferred_element_type=F32)


def iota(shape, dim):
    return lax.broadcasted_iota(jnp.int32, shape, dim)


def prep_kernel(perm_ref, cf_ref, cm_ref, cl_ref, w1_ref, wm_ref, wl_ref):
    own = lax.axis_index("rows")

    def strip(tap_of, a, h_in, eye):
        rows = []
        for e in (1, 0, -1):
            for h_out in (0, 1):
                rows.append(tap_of(9 * a + 3 * (h_in - h_out + 1) + (e + 1)))
        rows.append(jnp.zeros((64, rows[0].shape[1]), BF))
        return dot(eye, jnp.concatenate(rows, axis=0), NT)

    def halves(base):
        turned = pltpu.roll(base, 64, axis=1)
        found = {1: base[:, :128], -1: base[:, 128:], 2: turned[:, :128], 0: turned[:, 128:]}
        return {w_in: part.astype(BF) for w_in, part in found.items()}

    def fill(ref, at, parts, rows, bases):
        for d_in in (0, 1):
            for w_in in range(-1, 3):
                for base in bases:
                    row = base + at(d_in, w_in)
                    for place, rel in enumerate((0, 1, 2, -1)):
                        a = d_in - rel + 1
                        block = parts[a][w_in] if 0 <= a <= 2 else jnp.zeros((rows, 128), BF)
                        ref[row : row + rows, 128 * place : 128 * place + 128] = block

    def main_row(d_in, w_in):
        return 128 * d_in + {0: 0, 1: 64, 2: 256, -1: 320}[w_in]

    def rest_row(d_in, w_in):
        return 512 + 32 * d_in + {0: 0, 1: 16, 2: 64, -1: 80}[w_in]

    def eye_of(n):
        return (iota((n, n), 0) == iota((n, n), 1)).astype(F32).astype(BF)

    eye40, eye32 = eye_of(40), eye_of(32)
    main, rest = [], []
    for a in range(3):
        parts = [strip(lambda t: cf_ref[t], a, h_in, eye40) for h_in in (0, 1)]
        main.append(halves(jnp.concatenate([p[:32] for p in parts], axis=0)))
        rest.append(halves(jnp.concatenate([p[32:] for p in parts], axis=0)))
    fill(w1_ref, main_row, main, 64, (0,))
    fill(w1_ref, rest_row, rest, 16, (0,))
    for layer in range(2):
        main = [
            halves(
                jnp.concatenate(
                    [strip(lambda t: cm_ref[layer, t], a, h_in, eye32) for h_in in (0, 1)], axis=0
                )
            )
            for a in range(3)
        ]
        fill(wm_ref.at[layer], main_row, main, 64, (0, 512))
    clt = dot(eye32, cl_ref[...], NT).astype(BF)
    lane = iota((27, 128), 1)
    rel = jnp.where(lane < 32, 0, jnp.where(lane < 64, 2, jnp.where(lane < 96, 1, -1)))
    for d_in in (0, 1):
        for w_in in range(-1, 3):
            for h_in in (0, 1):
                a, e, b = d_in - rel, w_in - lane % 32, h_in - own
                tap = 9 * (a + 1) + 3 * (b + 1) + (e + 1)
                ok = (lane % 32 < 2) & (a >= -1) & (a <= 1) & (e >= -1) & (e <= 1) & (b >= -1) & (b <= 1)
                pick = (ok & (iota((27, 128), 0) == tap)).astype(F32).astype(BF)
                block = dot(clt, pick).astype(BF)
                row = main_row(d_in, w_in) + 32 * h_in
                wl_ref[row : row + 32] = block
                wl_ref[512 + row : 544 + row] = block


def perm_kernel(perm_ref):
    own = lax.axis_index("rows")
    lane = iota((1, 512), 1)
    src = (((lane // 32) % 2) ^ own) * 320 + (lane % 32) * 8 + lane // 64
    perm_ref[:, :512] = (iota((640, 512), 0) == src).astype(F32).astype(BF)
    lane = iota((1, 512), 1)
    src = (((lane // 8) % 2) ^ own) * 320 + (32 + lane % 8) * 8 + (lane // 128) * 2 + (lane // 64) % 2
    perm_ref[:, 512:] = (iota((640, 512), 0) == src).astype(F32).astype(BF)


def prep(cf, cm, cl):
    vm = pl.BlockSpec(memory_space=pltpu.VMEM)
    perm = pl.pallas_call(
        perm_kernel,
        out_shape=jax.ShapeDtypeStruct((640, 1024), BF),
        out_specs=vm,
        compiler_params=pltpu.CompilerParams(vmem_limit_bytes=8 * 2**20),
        cost_estimate=pl.CostEstimate(flops=10**9, bytes_accessed=3 * 10**6, transcendentals=0),
        name="perm",
    )()
    ws = pl.pallas_call(
        prep_kernel,
        out_shape=(
            jax.ShapeDtypeStruct((640, 512), BF),
            jax.ShapeDtypeStruct((2, 1024, 512), BF),
            jax.ShapeDtypeStruct((1024, 128), BF),
        ),
        in_specs=[vm] * 4,
        out_specs=[vm] * 3,
        compiler_params=pltpu.CompilerParams(vmem_limit_bytes=16 * 2**20),
        cost_estimate=pl.CostEstimate(flops=2 * 10**9, bytes_accessed=4 * 10**6, transcendentals=0),
        name="prep",
    )(perm, cf, cm, cl)
    return (*ws, perm)


def main_body(load_r, load_l, w1_ref, wm_ref, wl_ref, perm_ref, out_ref, win, rs, lp, xb1, xb, xb2, xb3):
    z = lax.axis_index("disp")
    core = lax.axis_index("cols")
    piece = core * 4 + z
    win[...] = jnp.zeros_like(win)

    def put(row, part):
        win[row : row + part.shape[0]] = part

    put(0, load_r(1, 0, 16))
    put(16, load_r(-3, 16, 32))
    put(32, load_r(-2, 0, 32))
    put(64, load_r(-1, 0, 32))
    put(96, load_r(0, 0, 32))
    put(136, load_l(-1))
    put(144, load_l(0))
    put(176, load_l(1))
    zp = dot(win[...], perm_ref[...])
    halfway = iota((128, 128), 1) < 64
    near_half, far_half = [], []
    for tile in range(4):
        straight = zp[:, 128 * tile : 128 * tile + 128]
        turned = pltpu.roll(straight, 64, axis=1)
        for even, a, b in ((0, straight, turned), (1, turned, straight)):
            near_half.append(jnp.where(halfway, a[:128], 0.0).astype(BF))
            far_half.append(jnp.where(halfway, 0.0, b[:128]).astype(BF))
            lp[2 * tile + even] = jnp.where(halfway[:64], a[128:], b[128:])
    for tile in range(4):
        lp[8 + tile] = zp[128:, 512 + 128 * tile : 640 + 128 * tile]
    zm = jnp.concatenate(
        [jnp.concatenate(near_half, axis=1), jnp.concatenate(far_half, axis=1)], axis=0
    )
    zpr = zp[:128]
    lane = iota((128, 512), 1)
    ze = jnp.concatenate(
        [jnp.where((lane // 16) % 4 == ww, zpr[:, 512:], 0.0).astype(BF) for ww in range(4)], axis=0
    )
    s, q = iota((112, 256), 0), iota((112, 256), 1)
    r = q % 128
    rel = jnp.where(r < 16, 32 + r, r - 96)
    dd = jnp.where(s < 56, 0, 1)
    pick = (rel == 36 + q // 128 - dd - 2 * (s - 56 * dd)).astype(F32).astype(BF)
    rsm = dot(pick, zm)
    s, q = iota((56, 512), 0), iota((56, 512), 1)
    r = q % 128
    rel = jnp.where(r < 16, 32 + r, r - 96)
    pick = (rel == 36 + (q // 128) % 2 - q // 256 - 2 * s).astype(F32).astype(BF)
    rse = dot(pick, ze)
    for tile in range(8):
        rs[tile] = rsm[:, 128 * tile : 128 * tile + 128]
    for tile in range(4):
        rs[8 + tile, 0:56] = rse[:, 128 * tile : 128 * tile + 128]

    def left_row(tile, column):
        for first, row in ((36, 48), (4, 16), (0, 12)):
            if column >= first:
                at = row + column - first
                return lp[tile, at : at + 1]

    lane = iota((32, 128), 1)
    low, even = lane < 64, (lane // 16) % 2 == 0
    depth = iota((32, 128), 0)
    nothing = jnp.zeros((32, 128), BF)
    first_ok = piece > 0
    last_ok = piece < 4 * lax.axis_size("cols") - 1

    def before(tile):
        return jnp.where(depth == 0, 0.0, pltpu.roll(tile, 1, axis=0))

    def after(tile):
        return jnp.where(depth == 31, 0.0, pltpu.roll(tile, 31, axis=0))

    class Rows:
        def __init__(self, out, own_lanes, halo_lanes, pick):
            self.out, self.own, self.halo, self.pick = out, own_lanes, halo_lanes, pick
            self.last, self.prior = None, None

        def push(self, block, values):
            if self.last is not None:
                self._halo(block - 1, values)
            here = slice(32 * block, 32 * block + 32)
            if self.own is not None:
                for lanes, value in zip(self.own, values):
                    self.out[here, lanes : lanes + 128] = value
            self.prior, self.last = self.last, values
            self.block = block

        def end(self):
            self._halo(self.block, [nothing] * len(self.last))

        def _halo(self, block, following):
            here = slice(32 * block, 32 * block + 32)
            prior = self.prior or [nothing] * len(following)
            for lanes, a, b, c in zip(self.halo, prior, self.last, following):
                self.out[here, lanes : lanes + 128] = self.pick(a, b, c)

    def beside(a, b, c):
        return jnp.where(low, c, a)

    def around(a, b, c):
        return jnp.where(low, b, jnp.where(even, c, a))

    volume = Rows(xb1, (0, 128), (256, 384), beside)
    remainder = Rows(xb1, None, (512,), around)
    for w2 in range(20):
        start = 20 - w2
        tiles = []
        for dd in range(2):
            acc = None
            for c in range(8):
                left = jnp.where(low, left_row(c, 2 * w2), left_row(c, 2 * w2 + 1))
                term = left * rs[c, 56 * dd + start : 56 * dd + start + 32]
                acc = term if acc is None else acc + term
            tiles.append(acc * 0.125)
        acc = None
        for c in range(4):
            left = jnp.where(even, left_row(8 + c, 2 * w2), left_row(8 + c, 2 * w2 + 1))
            term = left * rs[8 + c, start : start + 32]
            acc = term if acc is None else acc + term
        rest = (acc + pltpu.roll(acc, 64, axis=1)) * 0.125
        volume.push(w2, [tile.astype(BF) for tile in tiles])
        remainder.push(w2, [rest.astype(BF)])
    volume.end()
    remainder.end()


    class Layer:
        def __init__(self, x, weights, out, cuts):
            own = (0, 128, 512, 640)
            self.rows = Rows(out, own, [lanes + 256 for lanes in own], beside)
            self.x, self.weights = x, weights
            self.chunks = list(zip(cuts, cuts[1:]))

        def step(self):
            first, stop = self.chunks.pop(0)
            y = dot(self.x[32 * first : 32 * stop], self.weights[...])
            for w2 in range(first, stop):
                here = y[32 * (w2 - first) : 32 * (w2 - first) + 32]
                tiles = [
                    here[:, :128] + before(here[:, 256:384]),
                    here[:, 128:256] + after(here[:, 384:]),
                ]
                tiles = [jnp.maximum(tile, 0.0) for tile in tiles]
                if w2 < 2:
                    tiles = [jnp.where(first_ok, tile, 0.0) for tile in tiles]
                if w2 > 17:
                    tiles = [jnp.where(last_ok, tile, 0.0) for tile in tiles]
                high = [tile.astype(BF) for tile in tiles]
                rest = [(tile - part.astype(F32)).astype(BF) for tile, part in zip(tiles, high)]
                self.rows.push(w2, high + rest)
            if not self.chunks:
                self.rows.end()

    layers = [
        Layer(xb1, w1_ref, xb, (0, 7, 14, 20)),
        Layer(xb, wm_ref.at[0], xb2, (1, 6, 13, 19)),
        Layer(xb2, wm_ref.at[1], xb3, (1, 5, 12, 19)),
    ]
    for each in layers:
        for _ in range(len(each.chunks)):
            each.step()
    y = dot(xb3[64:576], wl_ref[...])
    cost = jnp.zeros((32, 128), F32)
    for w2 in range(16):
        part = y[32 * w2 : 32 * w2 + 32]
        part = part if w2 == 0 else pltpu.roll(part, 2 * w2, axis=1)
        cost = jnp.where((lane % 32) // 2 == w2, part, cost)
    moved = jnp.where(low, before(cost), after(cost))
    cost = cost + pltpu.roll(moved, 96, axis=1)
    top = jnp.max(cost, axis=0, keepdims=True)
    top = jnp.maximum(top, pltpu.roll(top, 64, axis=1))
    weight = jnp.exp(cost - top)
    level = (2 * depth + jnp.where(low, 0, 1)).astype(F32) * (1.0 / 64)
    upper = jnp.sum(weight * level, axis=0, keepdims=True)
    under = jnp.sum(weight, axis=0, keepdims=True)
    est = (upper + pltpu.roll(upper, 64, axis=1)) / (under + pltpu.roll(under, 64, axis=1))
    out_ref[...] = est[:, :32]


SCRATCH = [
    pltpu.VMEM((192, 640), BF),
    pltpu.VMEM((12, 112, 128), F32),
    pltpu.VMEM((12, 64, 128), F32),
    pltpu.VMEM((640, 640), BF),
    pltpu.VMEM((640, 1024), BF),
    pltpu.VMEM((640, 1024), BF),
    pltpu.VMEM((640, 1024), BF),
]


def joined(out_ref, first, s_ref, t_ref):
    for half, ref in enumerate((s_ref, t_ref)):
        lanes = slice(320 * half, 320 * half + 320)
        left = ref[1]
        out_ref[first + (slice(0, 32), lanes)] = ref[0]
        out_ref[first + (slice(32, 40), lanes)] = jnp.concatenate([left[:4], left[28:]], axis=0)


def pack_kernel(s_ref, t_ref, own_ref, edge_ref, rights_ref):
    joined(edge_ref, (), s_ref, t_ref)
    for half, ref in enumerate((s_ref, t_ref)):
        lanes = slice(320 * half, 320 * half + 320)
        own_ref[0:32, lanes] = ref[0]
        own_ref[32:64, lanes] = ref[1]
        rights_ref[:, lanes] = ref[0]


def pack(s, t):
    vm = pl.BlockSpec(memory_space=pltpu.VMEM)
    return pl.pallas_call(
        pack_kernel,
        out_shape=[jax.ShapeDtypeStruct((rows, 640), BF) for rows in (64, 40, 32)],
        in_specs=[vm] * 2,
        out_specs=[vm] * 3,
        compiler_params=pltpu.CompilerParams(vmem_limit_bytes=2**20),
        name="pack",
    )(s, t)


def collect_kernel(one_ref, two_ref, s_ref, t_ref, out_ref):
    out_ref[0] = one_ref[...]
    out_ref[1, 0:32] = two_ref[...]
    out_ref[1, 32:40] = jnp.zeros((8, 640), BF)
    joined(out_ref, (2,), s_ref, t_ref)


def collect(*parts):
    vm = pl.BlockSpec(memory_space=pltpu.VMEM)
    return pl.pallas_call(
        collect_kernel,
        out_shape=jax.ShapeDtypeStruct((3, 40, 640), BF),
        in_specs=[vm] * 4,
        out_specs=vm,
        compiler_params=pltpu.CompilerParams(vmem_limit_bytes=2**20),
        name="collect",
    )(*parts)


def stage_kernel(s_ref, out_ref):
    out_ref[...] = s_ref[...]


def stage(s):
    vm = pl.BlockSpec(memory_space=pltpu.VMEM)
    return pl.pallas_call(
        stage_kernel,
        out_shape=jax.ShapeDtypeStruct(s.shape, BF),
        in_specs=[vm],
        out_specs=vm,
        compiler_params=pltpu.CompilerParams(vmem_limit_bytes=2**20),
        cost_estimate=pl.CostEstimate(flops=10**9, bytes_accessed=10**6, transcendentals=0),
        name="stage",
    )(s)


def main_kernel(own, other, near, far, w1, wm, wl, perm, out, win, rs, lp, xb1, xb, xb2, xb3):
    z, core = lax.axis_index("disp"), lax.axis_index("cols")
    piece = core * 4 + z

    def load(dp, lo, hi):
        row = jnp.where(iota((hi - lo, 640), 1) < 320, 0, 1)
        if dp == 0:
            return jnp.where(row == 0, own[lo:hi], other[lo:hi])
        want = piece + dp
        ok = (want >= 0) & (want < 8)
        want = jnp.clip(want, 0, 7)
        turn = jnp.maximum((z ^ (want % 4)) - 1, 0)
        flip = core ^ (want // 4)
        part = jnp.where(row == flip, far[turn, lo:hi], near[turn, lo:hi])
        return jnp.where(ok, part, jnp.zeros((), BF))

    def left(dp):
        return load(dp, 32, 64) if dp == 0 else load(dp, 32, 40)

    main_body(load, left, w1, wm, wl, perm, out, win, rs, lp, xb1, xb, xb2, xb3)


def crossed(v, axis, k):
    count = lax.axis_size(axis)
    pairs = [(2 * i + c, 2 * (i ^ k) + 1 - c) for i in range(count) for c in (0, 1)]
    return lax.ppermute(v, (axis, "cols"), pairs)


def fast(left_feat, right_feat, conv_first, conv_mid, conv_last):
    zero = jnp.zeros((), BF)
    none = (0, 0, 0)
    s = lax.pad(right_feat, zero, ((0, 1, 0), none, none)) + lax.pad(
        left_feat, zero, ((1, 0, 0), none, none)
    )
    t = crossed(s, "rows", 1)
    s_3 = crossed(stage(s), "disp", 3)
    own, edge, rights = pack(s, t)
    swap = [(0, 1), (1, 0)]
    from_1 = crossed(edge, "disp", 1)
    from_2 = crossed(rights, "disp", 2)
    t_3 = crossed(s_3, "rows", 1)
    ws = prep(conv_first, conv_mid, conv_last.reshape(27, 32))
    other = lax.ppermute(own, "cols", swap)
    ws, from_1, from_2, s_3, t_3, other = lax.optimization_barrier(
        (ws, from_1, from_2, s_3, t_3, other)
    )
    near = collect(from_1, from_2, s_3, t_3)
    far = lax.ppermute(near, "cols", swap)
    vm = pl.BlockSpec(memory_space=pltpu.VMEM)
    return pl.pallas_call(
        main_kernel,
        out_shape=jax.ShapeDtypeStruct((1, 32), F32),
        in_specs=[vm] * 8,
        out_specs=vm,
        scratch_shapes=SCRATCH,
        compiler_params=pltpu.CompilerParams(vmem_limit_bytes=24 * 2**20),
        name="cost_volume",
    )(own, other, near, far, *ws)


def shards(left_feat, right_feat, conv_first, conv_mid, conv_last):
    sizes = tuple(lax.axis_size(name) for name in ("disp", "rows", "cols"))
    if sizes == (4, 2, 2) and left_feat.shape == (1, 32, 320) and conv_first.shape == (27, 32, 40):
        return fast(left_feat, right_feat, conv_first, conv_mid, conv_last)
    return general(left_feat, right_feat, conv_first, conv_mid, conv_last)


def solution(mesh):
    return jax.shard_map(
        shards,
        mesh=mesh,
        in_specs=(
            P(("tiles", "rows"), ("cols", "disp"), None),
            P(("tiles", "rows"), ("cols", "disp"), None),
            P(),
            P(),
            P(),
        ),
        out_specs=P(("tiles", "rows"), ("cols", "disp")),
        check_vma=False,
    )
```

```python
import jax
import jax.numpy as jnp
from jax import lax
from jax.experimental import pallas as pl
from jax.experimental.pallas import tpu as pltpu
from jax.sharding import PartitionSpec as P

MID = 2
DDEV = 16


def extended_2(block, sides, width):
    for axis, dim in sides:
        count = lax.axis_size(axis)
        forward = [(i, i + 1) for i in range(count - 1)]
        backward = [(target, source) for source, target in forward]
        low = lax.ppermute(
            lax.slice_in_dim(block, block.shape[dim] - width, None, axis=dim), axis, forward
        )
        high = lax.ppermute(lax.slice_in_dim(block, 0, width, axis=dim), axis, backward)
        block = jnp.concatenate([low, block, high], axis=dim)
    return block


def passed_along(x, axis, by):
    peers = lax.axis_size(axis)
    pairs = [(i, i + by) for i in range(peers) if 0 <= i + by < peers]
    return lax.ppermute(x, axis, pairs)


def combined_all(part, axis, combine):
    gathered = jax.tree.map(lambda a: lax.all_gather(a, axis), part)

    def take(source):
        return jax.tree.map(lambda a: lax.dynamic_index_in_dim(a, source, 0, False), gathered)

    return lax.fori_loop(
        1, lax.axis_size(axis), lambda source, state: combine(state, take(source)), take(0)
    )


def correlate(left_full, extended, groups, first_disp, count, total_disp):
    rows_here, width_here, channels = left_full.shape
    group_size = channels // groups
    left_groups = left_full.reshape(rows_here, width_here, groups, group_size)

    def single(offset):
        disp_value = first_disp + offset
        shifted = lax.dynamic_slice_in_dim(extended, 2 * width_here - disp_value, width_here, 1)
        right_groups = shifted.reshape(rows_here, width_here, groups, group_size)
        corr = (
            jnp.einsum(
                "hwgc,hwgc->ghw", left_groups, right_groups, preferred_element_type=jnp.float32
            )
            / group_size
        )
        inside = (disp_value >= 0) & (disp_value < total_disp)
        return jnp.where(inside, corr, 0.0).astype(jnp.bfloat16)

    return lax.map(single, jnp.arange(count, dtype=jnp.int32))


def convolve(padded, kernel):
    depth_out = padded.shape[0] - 2
    in_chans = padded.shape[1]
    rows_out = padded.shape[2] - 2
    cols_out = padded.shape[3] - 2
    out_chans = kernel.shape[1]
    columns = jnp.concatenate(
        [
            padded[:, :, row_tap : row_tap + rows_out, col_tap : col_tap + cols_out]
            for row_tap in range(3)
            for col_tap in range(3)
        ],
        axis=1,
    )
    flat = columns.reshape(depth_out + 2, 9 * in_chans, rows_out * cols_out)
    summed = jnp.zeros((depth_out, out_chans, rows_out * cols_out), jnp.float32)
    for disp_tap in range(3):
        taps = (
            jnp.transpose(kernel[9 * disp_tap : 9 * disp_tap + 9], (1, 0, 2))
            .reshape(out_chans, 9 * in_chans)
            .astype(flat.dtype)
        )
        summed = summed + jnp.einsum(
            "ok,dkn->don",
            taps,
            flat[disp_tap : disp_tap + depth_out],
            preferred_element_type=jnp.float32,
            precision=lax.Precision.HIGHEST,
        )
    return summed.reshape(depth_out, out_chans, rows_out, cols_out)


def widen(hidden):
    return extended_2(hidden, (("disp", 0), ("rows", 2), ("cols", 3)), 1)


def combine_parts(earlier, later):
    highest = jnp.maximum(earlier[0], later[0])
    scale_one = jnp.exp(earlier[0] - highest)
    scale_two = jnp.exp(later[0] - highest)
    return (
        highest,
        earlier[1] * scale_one + later[1] * scale_two,
        earlier[2] * scale_one + later[2] * scale_two,
    )


def general(left_feat, right_feat, conv_first, conv_mid, conv_last):
    piece_width = left_feat.shape[1]
    groups = conv_first.shape[2]
    disp_count = lax.axis_size("disp")
    depth_here = DDEV
    total_disp = depth_here * disp_count
    first_disp = lax.axis_index("disp") * depth_here
    left_full, right_full = (
        lax.all_gather(left_feat, "disp", axis=1, tiled=True),
        lax.all_gather(right_feat, "disp", axis=1, tiled=True),
    )
    prior_full = passed_along(right_full, "cols", 1)
    extended = jnp.concatenate([jnp.zeros_like(right_full), prior_full, right_full], axis=1)
    volume = correlate(left_full, extended, groups, first_disp, depth_here, total_disp)
    padded = extended_2(volume, (("disp", 0), ("rows", 2), ("cols", 3)), 1)
    hidden = jax.nn.relu(convolve(padded, conv_first))
    for layer in range(MID):
        hidden = jax.nn.relu(convolve(widen(hidden), conv_mid[layer]))
    cost_cube = convolve(widen(hidden), conv_last)[:, 0]
    levels = (
        (first_disp + jnp.arange(depth_here, dtype=jnp.int32)).astype(jnp.float32) / total_disp
    )[:, None, None]
    local_high = jnp.max(cost_cube, axis=0)
    weights = jnp.exp(cost_cube - local_high[None])
    merged = combined_all(
        (local_high, jnp.sum(weights, axis=0), jnp.sum(weights * levels, axis=0)),
        "disp",
        combine_parts,
    )
    whole_row = merged[2] / merged[1]
    return lax.dynamic_slice_in_dim(whole_row, lax.axis_index("disp") * piece_width, piece_width, 1)


BF, F32 = jnp.bfloat16, jnp.float32
NT = (((1,), (1,)), ((), ()))


def dot(a, b, dims=(((1,), (0,)), ((), ()))):
    return lax.dot_general(a, b, dims, preferred_element_type=F32)


def iota(shape, dim):
    return lax.broadcasted_iota(jnp.int32, shape, dim)


def prep_kernel(perm_ref, cf_ref, cm_ref, cl_ref, w1_ref, wm_ref, wl_ref):
    own = lax.axis_index("rows")

    def strip(tap_of, a, h_in, eye):
        rows = []
        for e in (1, 0, -1):
            for h_out in (0, 1):
                rows.append(tap_of(9 * a + 3 * (h_in - h_out + 1) + (e + 1)))
        rows.append(jnp.zeros((64, rows[0].shape[1]), BF))
        return dot(eye, jnp.concatenate(rows, axis=0), NT)

    def halves(base):
        turned = pltpu.roll(base, 64, axis=1)
        found = {1: base[:, :128], -1: base[:, 128:], 2: turned[:, :128], 0: turned[:, 128:]}
        return {w_in: part.astype(BF) for w_in, part in found.items()}

    def fill(ref, at, parts, rows, bases):
        for d_in in (0, 1):
            for w_in in range(-1, 3):
                for base in bases:
                    row = base + at(d_in, w_in)
                    for place, rel in enumerate((0, 1, 2, -1)):
                        a = d_in - rel + 1
                        block = parts[a][w_in] if 0 <= a <= 2 else jnp.zeros((rows, 128), BF)
                        ref[row : row + rows, 128 * place : 128 * place + 128] = block

    def main_row(d_in, w_in):
        return 128 * d_in + {0: 0, 1: 64, 2: 256, -1: 320}[w_in]

    def rest_row(d_in, w_in):
        return 512 + 32 * d_in + {0: 0, 1: 16, 2: 64, -1: 80}[w_in]

    def eye_of(n):
        return (iota((n, n), 0) == iota((n, n), 1)).astype(F32).astype(BF)

    eye40, eye32 = eye_of(40), eye_of(32)
    main, rest = [], []
    for a in range(3):
        parts = [strip(lambda t: cf_ref[t], a, h_in, eye40) for h_in in (0, 1)]
        main.append(halves(jnp.concatenate([p[:32] for p in parts], axis=0)))
        rest.append(halves(jnp.concatenate([p[32:] for p in parts], axis=0)))
    fill(w1_ref, main_row, main, 64, (0,))
    fill(w1_ref, rest_row, rest, 16, (0,))
    for layer in range(2):
        main = [
            halves(
                jnp.concatenate(
                    [strip(lambda t: cm_ref[layer, t], a, h_in, eye32) for h_in in (0, 1)], axis=0
                )
            )
            for a in range(3)
        ]
        fill(wm_ref.at[layer], main_row, main, 64, (0, 512))
    clt = dot(eye32, cl_ref[...], NT).astype(BF)
    lane = iota((27, 128), 1)
    rel = jnp.where(lane < 32, 0, jnp.where(lane < 64, 2, jnp.where(lane < 96, 1, -1)))
    for d_in in (0, 1):
        for w_in in range(-1, 3):
            for h_in in (0, 1):
                a, e, b = d_in - rel, w_in - lane % 32, h_in - own
                tap = 9 * (a + 1) + 3 * (b + 1) + (e + 1)
                ok = (lane % 32 < 2) & (a >= -1) & (a <= 1) & (e >= -1) & (e <= 1) & (b >= -1) & (b <= 1)
                pick = (ok & (iota((27, 128), 0) == tap)).astype(F32).astype(BF)
                block = dot(clt, pick).astype(BF)
                row = main_row(d_in, w_in) + 32 * h_in
                wl_ref[row : row + 32] = block
                wl_ref[512 + row : 544 + row] = block


def perm_kernel(perm_ref):
    own = lax.axis_index("rows")
    lane = iota((1, 512), 1)
    src = (((lane // 32) % 2) ^ own) * 320 + (lane % 32) * 8 + lane // 64
    perm_ref[:, :512] = (iota((640, 512), 0) == src).astype(F32).astype(BF)
    lane = iota((1, 512), 1)
    src = (((lane // 8) % 2) ^ own) * 320 + (32 + lane % 8) * 8 + (lane // 128) * 2 + (lane // 64) % 2
    perm_ref[:, 512:] = (iota((640, 512), 0) == src).astype(F32).astype(BF)


def prep(cf, cm, cl):
    vm = pl.BlockSpec(memory_space=pltpu.VMEM)
    perm = pl.pallas_call(
        perm_kernel,
        out_shape=jax.ShapeDtypeStruct((640, 1024), BF),
        out_specs=vm,
        compiler_params=pltpu.CompilerParams(vmem_limit_bytes=8 * 2**20),
        cost_estimate=pl.CostEstimate(flops=10**9, bytes_accessed=3 * 10**6, transcendentals=0),
        name="perm",
    )()
    ws = pl.pallas_call(
        prep_kernel,
        out_shape=(
            jax.ShapeDtypeStruct((640, 512), BF),
            jax.ShapeDtypeStruct((2, 1024, 512), BF),
            jax.ShapeDtypeStruct((1024, 128), BF),
        ),
        in_specs=[vm] * 4,
        out_specs=[vm] * 3,
        compiler_params=pltpu.CompilerParams(vmem_limit_bytes=16 * 2**20),
        cost_estimate=pl.CostEstimate(flops=2 * 10**9, bytes_accessed=4 * 10**6, transcendentals=0),
        name="prep",
    )(perm, cf, cm, cl)
    return (*ws, perm)


def main_body(load_r, load_l, w1_ref, wm_ref, wl_ref, perm_ref, out_ref, win, rs, lp, xb1, xb, xb2, xb3):
    z = lax.axis_index("disp")
    core = lax.axis_index("cols")
    piece = core * 4 + z
    win[...] = jnp.zeros_like(win)

    def put(row, part):
        win[row : row + part.shape[0]] = part

    put(0, load_r(1, 0, 16))
    put(16, load_r(-3, 16, 32))
    put(32, load_r(-2, 0, 32))
    put(64, load_r(-1, 0, 32))
    put(96, load_r(0, 0, 32))
    put(136, load_l(-1))
    put(144, load_l(0))
    put(176, load_l(1))
    zp = dot(win[...], perm_ref[...])
    halfway = iota((128, 128), 1) < 64
    near_half, far_half = [], []
    for tile in range(4):
        straight = zp[:, 128 * tile : 128 * tile + 128]
        turned = pltpu.roll(straight, 64, axis=1)
        for even, a, b in ((0, straight, turned), (1, turned, straight)):
            near_half.append(jnp.where(halfway, a[:128], 0.0).astype(BF))
            far_half.append(jnp.where(halfway, 0.0, b[:128]).astype(BF))
            lp[2 * tile + even] = jnp.where(halfway[:64], a[128:], b[128:])
    for tile in range(4):
        lp[8 + tile] = zp[128:, 512 + 128 * tile : 640 + 128 * tile]
    zm = jnp.concatenate(
        [jnp.concatenate(near_half, axis=1), jnp.concatenate(far_half, axis=1)], axis=0
    )
    zpr = zp[:128]
    lane = iota((128, 512), 1)
    ze = jnp.concatenate(
        [jnp.where((lane // 16) % 4 == ww, zpr[:, 512:], 0.0).astype(BF) for ww in range(4)], axis=0
    )
    s, q = iota((112, 256), 0), iota((112, 256), 1)
    r = q % 128
    rel = jnp.where(r < 16, 32 + r, r - 96)
    dd = jnp.where(s < 56, 0, 1)
    pick = (rel == 36 + q // 128 - dd - 2 * (s - 56 * dd)).astype(F32).astype(BF)
    rsm = dot(pick, zm)
    s, q = iota((56, 512), 0), iota((56, 512), 1)
    r = q % 128
    rel = jnp.where(r < 16, 32 + r, r - 96)
    pick = (rel == 36 + (q // 128) % 2 - q // 256 - 2 * s).astype(F32).astype(BF)
    rse = dot(pick, ze)
    for tile in range(8):
        rs[tile] = rsm[:, 128 * tile : 128 * tile + 128]
    for tile in range(4):
        rs[8 + tile, 0:56] = rse[:, 128 * tile : 128 * tile + 128]

    def left_row(tile, column):
        for first, row in ((36, 48), (4, 16), (0, 12)):
            if column >= first:
                at = row + column - first
                return lp[tile, at : at + 1]

    lane = iota((32, 128), 1)
    low, even = lane < 64, (lane // 16) % 2 == 0
    depth = iota((32, 128), 0)
    nothing = jnp.zeros((32, 128), BF)
    first_ok = piece > 0
    last_ok = piece < 4 * lax.axis_size("cols") - 1

    def before(tile):
        return jnp.where(depth == 0, 0.0, pltpu.roll(tile, 1, axis=0))

    def after(tile):
        return jnp.where(depth == 31, 0.0, pltpu.roll(tile, 31, axis=0))

    class Rows:
        def __init__(self, out, own_lanes, halo_lanes, pick):
            self.out, self.own, self.halo, self.pick = out, own_lanes, halo_lanes, pick
            self.last, self.prior = None, None

        def push(self, block, values):
            if self.last is not None:
                self._halo(block - 1, values)
            here = slice(32 * block, 32 * block + 32)
            if self.own is not None:
                for lanes, value in zip(self.own, values):
                    self.out[here, lanes : lanes + 128] = value
            self.prior, self.last = self.last, values
            self.block = block

        def end(self):
            self._halo(self.block, [nothing] * len(self.last))

        def _halo(self, block, following):
            here = slice(32 * block, 32 * block + 32)
            prior = self.prior or [nothing] * len(following)
            for lanes, a, b, c in zip(self.halo, prior, self.last, following):
                self.out[here, lanes : lanes + 128] = self.pick(a, b, c)

    def beside(a, b, c):
        return jnp.where(low, c, a)

    def around(a, b, c):
        return jnp.where(low, b, jnp.where(even, c, a))

    volume = Rows(xb1, (0, 128), (256, 384), beside)
    remainder = Rows(xb1, None, (512,), around)
    for w2 in range(20):
        start = 20 - w2
        tiles = []
        for dd in range(2):
            acc = None
            for c in range(8):
                left = jnp.where(low, left_row(c, 2 * w2), left_row(c, 2 * w2 + 1))
                term = left * rs[c, 56 * dd + start : 56 * dd + start + 32]
                acc = term if acc is None else acc + term
            tiles.append(acc * 0.125)
        acc = None
        for c in range(4):
            left = jnp.where(even, left_row(8 + c, 2 * w2), left_row(8 + c, 2 * w2 + 1))
            term = left * rs[8 + c, start : start + 32]
            acc = term if acc is None else acc + term
        rest = (acc + pltpu.roll(acc, 64, axis=1)) * 0.125
        volume.push(w2, [tile.astype(BF) for tile in tiles])
        remainder.push(w2, [rest.astype(BF)])
    volume.end()
    remainder.end()


    class Layer:
        def __init__(self, x, weights, out, cuts):
            own = (0, 128, 512, 640)
            self.rows = Rows(out, own, [lanes + 256 for lanes in own], beside)
            self.x, self.weights = x, weights
            self.chunks = list(zip(cuts, cuts[1:]))

        def step(self):
            first, stop = self.chunks.pop(0)
            y = dot(self.x[32 * first : 32 * stop], self.weights[...])
            for w2 in range(first, stop):
                here = y[32 * (w2 - first) : 32 * (w2 - first) + 32]
                tiles = [
                    here[:, :128] + before(here[:, 256:384]),
                    here[:, 128:256] + after(here[:, 384:]),
                ]
                tiles = [jnp.maximum(tile, 0.0) for tile in tiles]
                if w2 < 2:
                    tiles = [jnp.where(first_ok, tile, 0.0) for tile in tiles]
                if w2 > 17:
                    tiles = [jnp.where(last_ok, tile, 0.0) for tile in tiles]
                high = [tile.astype(BF) for tile in tiles]
                rest = [(tile - part.astype(F32)).astype(BF) for tile, part in zip(tiles, high)]
                self.rows.push(w2, high + rest)
            if not self.chunks:
                self.rows.end()

    layers = [
        Layer(xb1, w1_ref, xb, (0, 7, 14, 20)),
        Layer(xb, wm_ref.at[0], xb2, (1, 6, 13, 19)),
        Layer(xb2, wm_ref.at[1], xb3, (1, 5, 12, 19)),
    ]
    for each in layers:
        for _ in range(len(each.chunks)):
            each.step()
    y = dot(xb3[64:576], wl_ref[...])
    cost = jnp.zeros((32, 128), F32)
    for w2 in range(16):
        part = y[32 * w2 : 32 * w2 + 32]
        part = part if w2 == 0 else pltpu.roll(part, 2 * w2, axis=1)
        cost = jnp.where((lane % 32) // 2 == w2, part, cost)
    moved = jnp.where(low, before(cost), after(cost))
    cost = cost + pltpu.roll(moved, 96, axis=1)
    top = jnp.max(cost, axis=0, keepdims=True)
    top = jnp.maximum(top, pltpu.roll(top, 64, axis=1))
    weight = jnp.exp(cost - top)
    level = (2 * depth + jnp.where(low, 0, 1)).astype(F32) * (1.0 / 64)
    upper = jnp.sum(weight * level, axis=0, keepdims=True)
    under = jnp.sum(weight, axis=0, keepdims=True)
    est = (upper + pltpu.roll(upper, 64, axis=1)) / (under + pltpu.roll(under, 64, axis=1))
    out_ref[...] = est[:, :32]


SCRATCH = [
    pltpu.VMEM((192, 640), BF),
    pltpu.VMEM((12, 112, 128), F32),
    pltpu.VMEM((12, 64, 128), F32),
    pltpu.VMEM((640, 640), BF),
    pltpu.VMEM((640, 1024), BF),
    pltpu.VMEM((640, 1024), BF),
    pltpu.VMEM((640, 1024), BF),
]


def pack_kernel(s_ref, t_ref, own_ref, edge_ref, rights_ref):
    for half, ref in enumerate((s_ref, t_ref)):
        lanes = slice(320 * half, 320 * half + 320)
        right, left = ref[:, :320], ref[:, 320:]
        edge_ref[0:32, lanes] = right
        edge_ref[32:40, lanes] = jnp.concatenate([left[:4], left[28:]], axis=0)
        own_ref[0:32, lanes] = right
        own_ref[32:64, lanes] = left
        rights_ref[:, lanes] = right


def pack(s, t):
    vm = pl.BlockSpec(memory_space=pltpu.VMEM)
    return pl.pallas_call(
        pack_kernel,
        out_shape=[jax.ShapeDtypeStruct((rows, 640), BF) for rows in (64, 40, 32)],
        in_specs=[vm] * 2,
        out_specs=[vm] * 3,
        compiler_params=pltpu.CompilerParams(vmem_limit_bytes=2**20),
        name="pack",
    )(s, t)


def collect_kernel(one_ref, two_ref, s_ref, t_ref, out_ref):
    out_ref[0] = one_ref[...]
    out_ref[1, 0:32] = two_ref[...]
    out_ref[1, 32:40] = jnp.zeros((8, 640), BF)
    out_ref[2, :, 0:320] = s_ref[...]
    out_ref[2, :, 320:640] = t_ref[...]


def collect(*parts):
    vm = pl.BlockSpec(memory_space=pltpu.VMEM)
    return pl.pallas_call(
        collect_kernel,
        out_shape=jax.ShapeDtypeStruct((3, 40, 640), BF),
        in_specs=[vm] * 4,
        out_specs=vm,
        compiler_params=pltpu.CompilerParams(vmem_limit_bytes=2**20),
        name="collect",
    )(*parts)


def stage_kernel(s_ref, out_ref):
    left = s_ref[:, 320:]
    out_ref[0:32] = s_ref[:, :320]
    out_ref[32:40] = jnp.concatenate([left[:4], left[28:]], axis=0)


def stage(s):
    vm = pl.BlockSpec(memory_space=pltpu.VMEM)
    return pl.pallas_call(
        stage_kernel,
        out_shape=jax.ShapeDtypeStruct((40, 320), BF),
        in_specs=[vm],
        out_specs=vm,
        compiler_params=pltpu.CompilerParams(vmem_limit_bytes=2**20),
        cost_estimate=pl.CostEstimate(flops=10**9, bytes_accessed=10**6, transcendentals=0),
        name="stage",
    )(s)


def main_kernel(own, other, near, far, w1, wm, wl, perm, out, win, rs, lp, xb1, xb, xb2, xb3):
    z, core = lax.axis_index("disp"), lax.axis_index("cols")
    piece = core * 4 + z

    def load(dp, lo, hi):
        row = jnp.where(iota((hi - lo, 640), 1) < 320, 0, 1)
        if dp == 0:
            return jnp.where(row == 0, own[lo:hi], other[lo:hi])
        want = piece + dp
        ok = (want >= 0) & (want < 8)
        want = jnp.clip(want, 0, 7)
        turn = jnp.maximum((z ^ (want % 4)) - 1, 0)
        flip = core ^ (want // 4)
        part = jnp.where(row == flip, far[turn, lo:hi], near[turn, lo:hi])
        return jnp.where(ok, part, jnp.zeros((), BF))

    def left(dp):
        return load(dp, 32, 64) if dp == 0 else load(dp, 32, 40)

    main_body(load, left, w1, wm, wl, perm, out, win, rs, lp, xb1, xb, xb2, xb3)


def crossed(v, axis, k):
    count = lax.axis_size(axis)
    pairs = [(2 * i + c, 2 * (i ^ k) + 1 - c) for i in range(count) for c in (0, 1)]
    return lax.ppermute(v, (axis, "cols"), pairs)


def fast(left_feat, right_feat, conv_first, conv_mid, conv_last):
    zero = jnp.zeros((), BF)
    s = lax.pad(right_feat[0], zero, ((0, 0, 0), (0, 320, 0))) + lax.pad(
        left_feat[0], zero, ((0, 0, 0), (320, 0, 0))
    )
    t = crossed(s, "rows", 1)
    s_3 = crossed(stage(s), "disp", 3)
    own, edge, rights = pack(s, t)
    swap = [(0, 1), (1, 0)]
    from_1 = crossed(edge, "disp", 1)
    from_2 = crossed(rights, "disp", 2)
    other = lax.ppermute(own, "cols", swap)
    s_3, other = lax.optimization_barrier((s_3, other))
    t_3 = crossed(s_3, "rows", 1)
    ws = prep(conv_first, conv_mid, conv_last.reshape(27, 32))
    ws, from_1, from_2, s_3, t_3, other = lax.optimization_barrier(
        (ws, from_1, from_2, s_3, t_3, other)
    )
    near = collect(from_1, from_2, s_3, t_3)
    far = lax.ppermute(near, "cols", swap)
    vm = pl.BlockSpec(memory_space=pltpu.VMEM)
    return pl.pallas_call(
        main_kernel,
        out_shape=jax.ShapeDtypeStruct((1, 32), F32),
        in_specs=[vm] * 8,
        out_specs=vm,
        scratch_shapes=SCRATCH,
        compiler_params=pltpu.CompilerParams(vmem_limit_bytes=24 * 2**20),
        name="cost_volume",
    )(own, other, near, far, *ws)


def shards(left_feat, right_feat, conv_first, conv_mid, conv_last):
    sizes = tuple(lax.axis_size(name) for name in ("disp", "rows", "cols"))
    if sizes == (4, 2, 2) and left_feat.shape == (1, 32, 320) and conv_first.shape == (27, 32, 40):
        return fast(left_feat, right_feat, conv_first, conv_mid, conv_last)
    return general(left_feat, right_feat, conv_first, conv_mid, conv_last)


def solution(mesh):
    return jax.shard_map(
        shards,
        mesh=mesh,
        in_specs=(
            P(("tiles", "rows"), ("cols", "disp"), None),
            P(("tiles", "rows"), ("cols", "disp"), None),
            P(),
            P(),
            P(),
        ),
        out_specs=P(("tiles", "rows"), ("cols", "disp")),
        check_vma=False,
    )
```

```python
import jax
import jax.numpy as jnp
from jax import lax
from jax.experimental import pallas as pl
from jax.experimental.pallas import tpu as pltpu
from jax.sharding import PartitionSpec as P

MID = 2
DDEV = 16


def extended_2(block, sides, width):
    for axis, dim in sides:
        count = lax.axis_size(axis)
        forward = [(i, i + 1) for i in range(count - 1)]
        backward = [(target, source) for source, target in forward]
        low = lax.ppermute(
            lax.slice_in_dim(block, block.shape[dim] - width, None, axis=dim), axis, forward
        )
        high = lax.ppermute(lax.slice_in_dim(block, 0, width, axis=dim), axis, backward)
        block = jnp.concatenate([low, block, high], axis=dim)
    return block


def passed_along(x, axis, by):
    peers = lax.axis_size(axis)
    pairs = [(i, i + by) for i in range(peers) if 0 <= i + by < peers]
    return lax.ppermute(x, axis, pairs)


def combined_all(part, axis, combine):
    gathered = jax.tree.map(lambda a: lax.all_gather(a, axis), part)

    def take(source):
        return jax.tree.map(lambda a: lax.dynamic_index_in_dim(a, source, 0, False), gathered)

    return lax.fori_loop(
        1, lax.axis_size(axis), lambda source, state: combine(state, take(source)), take(0)
    )


def correlate(left_full, extended, groups, first_disp, count, total_disp):
    rows_here, width_here, channels = left_full.shape
    group_size = channels // groups
    left_groups = left_full.reshape(rows_here, width_here, groups, group_size)

    def single(offset):
        disp_value = first_disp + offset
        shifted = lax.dynamic_slice_in_dim(extended, 2 * width_here - disp_value, width_here, 1)
        right_groups = shifted.reshape(rows_here, width_here, groups, group_size)
        corr = (
            jnp.einsum(
                "hwgc,hwgc->ghw", left_groups, right_groups, preferred_element_type=jnp.float32
            )
            / group_size
        )
        inside = (disp_value >= 0) & (disp_value < total_disp)
        return jnp.where(inside, corr, 0.0).astype(jnp.bfloat16)

    return lax.map(single, jnp.arange(count, dtype=jnp.int32))


def convolve(padded, kernel):
    depth_out = padded.shape[0] - 2
    in_chans = padded.shape[1]
    rows_out = padded.shape[2] - 2
    cols_out = padded.shape[3] - 2
    out_chans = kernel.shape[1]
    columns = jnp.concatenate(
        [
            padded[:, :, row_tap : row_tap + rows_out, col_tap : col_tap + cols_out]
            for row_tap in range(3)
            for col_tap in range(3)
        ],
        axis=1,
    )
    flat = columns.reshape(depth_out + 2, 9 * in_chans, rows_out * cols_out)
    summed = jnp.zeros((depth_out, out_chans, rows_out * cols_out), jnp.float32)
    for disp_tap in range(3):
        taps = (
            jnp.transpose(kernel[9 * disp_tap : 9 * disp_tap + 9], (1, 0, 2))
            .reshape(out_chans, 9 * in_chans)
            .astype(flat.dtype)
        )
        summed = summed + jnp.einsum(
            "ok,dkn->don",
            taps,
            flat[disp_tap : disp_tap + depth_out],
            preferred_element_type=jnp.float32,
            precision=lax.Precision.HIGHEST,
        )
    return summed.reshape(depth_out, out_chans, rows_out, cols_out)


def widen(hidden):
    return extended_2(hidden, (("disp", 0), ("rows", 2), ("cols", 3)), 1)


def combine_parts(earlier, later):
    highest = jnp.maximum(earlier[0], later[0])
    scale_one = jnp.exp(earlier[0] - highest)
    scale_two = jnp.exp(later[0] - highest)
    return (
        highest,
        earlier[1] * scale_one + later[1] * scale_two,
        earlier[2] * scale_one + later[2] * scale_two,
    )


def general(left_feat, right_feat, conv_first, conv_mid, conv_last):
    piece_width = left_feat.shape[1]
    groups = conv_first.shape[2]
    disp_count = lax.axis_size("disp")
    depth_here = DDEV
    total_disp = depth_here * disp_count
    first_disp = lax.axis_index("disp") * depth_here
    left_full, right_full = (
        lax.all_gather(left_feat, "disp", axis=1, tiled=True),
        lax.all_gather(right_feat, "disp", axis=1, tiled=True),
    )
    prior_full = passed_along(right_full, "cols", 1)
    extended = jnp.concatenate([jnp.zeros_like(right_full), prior_full, right_full], axis=1)
    volume = correlate(left_full, extended, groups, first_disp, depth_here, total_disp)
    padded = extended_2(volume, (("disp", 0), ("rows", 2), ("cols", 3)), 1)
    hidden = jax.nn.relu(convolve(padded, conv_first))
    for layer in range(MID):
        hidden = jax.nn.relu(convolve(widen(hidden), conv_mid[layer]))
    cost_cube = convolve(widen(hidden), conv_last)[:, 0]
    levels = (
        (first_disp + jnp.arange(depth_here, dtype=jnp.int32)).astype(jnp.float32) / total_disp
    )[:, None, None]
    local_high = jnp.max(cost_cube, axis=0)
    weights = jnp.exp(cost_cube - local_high[None])
    merged = combined_all(
        (local_high, jnp.sum(weights, axis=0), jnp.sum(weights * levels, axis=0)),
        "disp",
        combine_parts,
    )
    whole_row = merged[2] / merged[1]
    return lax.dynamic_slice_in_dim(whole_row, lax.axis_index("disp") * piece_width, piece_width, 1)


BF, F32 = jnp.bfloat16, jnp.float32
NT = (((1,), (1,)), ((), ()))


def dot(a, b, dims=(((1,), (0,)), ((), ()))):
    return lax.dot_general(a, b, dims, preferred_element_type=F32)


def iota(shape, dim):
    return lax.broadcasted_iota(jnp.int32, shape, dim)


def prep_kernel(perm_ref, cf_ref, cm_ref, cl_ref, w1_ref, wm_ref, wl_ref):
    own = lax.axis_index("rows")

    def strip(tap_of, a, h_in, eye):
        rows = []
        for e in (1, 0, -1):
            for h_out in (0, 1):
                rows.append(tap_of(9 * a + 3 * (h_in - h_out + 1) + (e + 1)))
        rows.append(jnp.zeros((64, rows[0].shape[1]), BF))
        return dot(eye, jnp.concatenate(rows, axis=0), NT)

    def halves(base):
        turned = pltpu.roll(base, 64, axis=1)
        found = {1: base[:, :128], -1: base[:, 128:], 2: turned[:, :128], 0: turned[:, 128:]}
        return {w_in: part.astype(BF) for w_in, part in found.items()}

    def fill(ref, at, parts, rows, bases):
        for d_in in (0, 1):
            for w_in in range(-1, 3):
                for base in bases:
                    row = base + at(d_in, w_in)
                    for place, rel in enumerate((0, 1, 2, -1)):
                        a = d_in - rel + 1
                        block = parts[a][w_in] if 0 <= a <= 2 else jnp.zeros((rows, 128), BF)
                        ref[row : row + rows, 128 * place : 128 * place + 128] = block

    def main_row(d_in, w_in):
        return 128 * d_in + {0: 0, 1: 64, 2: 256, -1: 320}[w_in]

    def rest_row(d_in, w_in):
        return 512 + 32 * d_in + {0: 0, 1: 16, 2: 64, -1: 80}[w_in]

    def eye_of(n):
        return (iota((n, n), 0) == iota((n, n), 1)).astype(F32).astype(BF)

    eye40, eye32 = eye_of(40), eye_of(32)
    main, rest = [], []
    for a in range(3):
        parts = [strip(lambda t: cf_ref[t], a, h_in, eye40) for h_in in (0, 1)]
        main.append(halves(jnp.concatenate([p[:32] for p in parts], axis=0)))
        rest.append(halves(jnp.concatenate([p[32:] for p in parts], axis=0)))
    fill(w1_ref, main_row, main, 64, (0,))
    fill(w1_ref, rest_row, rest, 16, (0,))
    for layer in range(2):
        main = [
            halves(
                jnp.concatenate(
                    [strip(lambda t: cm_ref[layer, t], a, h_in, eye32) for h_in in (0, 1)], axis=0
                )
            )
            for a in range(3)
        ]
        fill(wm_ref.at[layer], main_row, main, 64, (0, 512))
    clt = dot(eye32, cl_ref[...], NT).astype(BF)
    lane = iota((27, 128), 1)
    rel = jnp.where(lane < 32, 0, jnp.where(lane < 64, 2, jnp.where(lane < 96, 1, -1)))
    for d_in in (0, 1):
        for w_in in range(-1, 3):
            for h_in in (0, 1):
                a, e, b = d_in - rel, w_in - lane % 32, h_in - own
                tap = 9 * (a + 1) + 3 * (b + 1) + (e + 1)
                ok = (lane % 32 < 2) & (a >= -1) & (a <= 1) & (e >= -1) & (e <= 1) & (b >= -1) & (b <= 1)
                pick = (ok & (iota((27, 128), 0) == tap)).astype(F32).astype(BF)
                block = dot(clt, pick).astype(BF)
                row = main_row(d_in, w_in) + 32 * h_in
                wl_ref[row : row + 32] = block
                wl_ref[512 + row : 544 + row] = block


def perm_kernel(perm_ref):
    own = lax.axis_index("rows")
    lane = iota((1, 512), 1)
    src = (((lane // 32) % 2) ^ own) * 320 + (lane % 32) * 8 + lane // 64
    perm_ref[:, :512] = (iota((640, 512), 0) == src).astype(F32).astype(BF)
    lane = iota((1, 512), 1)
    src = (((lane // 8) % 2) ^ own) * 320 + (32 + lane % 8) * 8 + (lane // 128) * 2 + (lane // 64) % 2
    perm_ref[:, 512:] = (iota((640, 512), 0) == src).astype(F32).astype(BF)


def prep(cf, cm, cl):
    vm = pl.BlockSpec(memory_space=pltpu.VMEM)
    perm = pl.pallas_call(
        perm_kernel,
        out_shape=jax.ShapeDtypeStruct((640, 1024), BF),
        out_specs=vm,
        compiler_params=pltpu.CompilerParams(vmem_limit_bytes=8 * 2**20),
        cost_estimate=pl.CostEstimate(flops=10**9, bytes_accessed=3 * 10**6, transcendentals=0),
        name="perm",
    )()
    ws = pl.pallas_call(
        prep_kernel,
        out_shape=(
            jax.ShapeDtypeStruct((640, 512), BF),
            jax.ShapeDtypeStruct((2, 1024, 512), BF),
            jax.ShapeDtypeStruct((1024, 128), BF),
        ),
        in_specs=[vm] * 4,
        out_specs=[vm] * 3,
        compiler_params=pltpu.CompilerParams(vmem_limit_bytes=16 * 2**20),
        cost_estimate=pl.CostEstimate(flops=2 * 10**9, bytes_accessed=4 * 10**6, transcendentals=0),
        name="prep",
    )(perm, cf, cm, cl)
    return (*ws, perm)


def main_body(load_r, load_l, w1_ref, wm_ref, wl_ref, perm_ref, out_ref, win, rs, lp, xb1, xb, xb2, xb3):
    z = lax.axis_index("disp")
    core = lax.axis_index("cols")
    piece = core * 4 + z
    win[...] = jnp.zeros_like(win)

    def put(row, part):
        win[row : row + part.shape[0]] = part

    put(0, load_r(1, 0, 16))
    put(16, load_r(-3, 16, 32))
    put(32, load_r(-2, 0, 32))
    put(64, load_r(-1, 0, 32))
    put(96, load_r(0, 0, 32))
    put(136, load_l(-1))
    put(144, load_l(0))
    put(176, load_l(1))
    zp = dot(win[...], perm_ref[...])
    halfway = iota((128, 128), 1) < 64
    near_half, far_half = [], []
    for tile in range(4):
        straight = zp[:, 128 * tile : 128 * tile + 128]
        turned = pltpu.roll(straight, 64, axis=1)
        for even, a, b in ((0, straight, turned), (1, turned, straight)):
            near_half.append(jnp.where(halfway, a[:128], 0.0).astype(BF))
            far_half.append(jnp.where(halfway, 0.0, b[:128]).astype(BF))
            lp[2 * tile + even] = jnp.where(halfway[:64], a[128:], b[128:])
    for tile in range(4):
        lp[8 + tile] = zp[128:, 512 + 128 * tile : 640 + 128 * tile]
    zm = jnp.concatenate(
        [jnp.concatenate(near_half, axis=1), jnp.concatenate(far_half, axis=1)], axis=0
    )
    zpr = zp[:128]
    lane = iota((128, 512), 1)
    ze = jnp.concatenate(
        [jnp.where((lane // 16) % 4 == ww, zpr[:, 512:], 0.0).astype(BF) for ww in range(4)], axis=0
    )
    s, q = iota((112, 256), 0), iota((112, 256), 1)
    r = q % 128
    rel = jnp.where(r < 16, 32 + r, r - 96)
    dd = jnp.where(s < 56, 0, 1)
    pick = (rel == 36 + q // 128 - dd - 2 * (s - 56 * dd)).astype(F32).astype(BF)
    rsm = dot(pick, zm)
    s, q = iota((56, 512), 0), iota((56, 512), 1)
    r = q % 128
    rel = jnp.where(r < 16, 32 + r, r - 96)
    pick = (rel == 36 + (q // 128) % 2 - q // 256 - 2 * s).astype(F32).astype(BF)
    rse = dot(pick, ze)
    for tile in range(8):
        rs[tile] = rsm[:, 128 * tile : 128 * tile + 128]
    for tile in range(4):
        rs[8 + tile, 0:56] = rse[:, 128 * tile : 128 * tile + 128]

    def left_row(tile, column):
        for first, row in ((36, 48), (4, 16), (0, 12)):
            if column >= first:
                at = row + column - first
                return lp[tile, at : at + 1]

    lane = iota((32, 128), 1)
    low, even = lane < 64, (lane // 16) % 2 == 0
    depth = iota((32, 128), 0)
    nothing = jnp.zeros((32, 128), BF)
    first_ok = piece > 0
    last_ok = piece < 4 * lax.axis_size("cols") - 1

    def before(tile):
        return jnp.where(depth == 0, 0.0, pltpu.roll(tile, 1, axis=0))

    def after(tile):
        return jnp.where(depth == 31, 0.0, pltpu.roll(tile, 31, axis=0))

    class Rows:
        def __init__(self, out, own_lanes, halo_lanes, pick):
            self.out, self.own, self.halo, self.pick = out, own_lanes, halo_lanes, pick
            self.last, self.prior = None, None

        def push(self, block, values):
            if self.last is not None:
                self._halo(block - 1, values)
            here = slice(32 * block, 32 * block + 32)
            if self.own is not None:
                for lanes, value in zip(self.own, values):
                    self.out[here, lanes : lanes + 128] = value
            self.prior, self.last = self.last, values
            self.block = block

        def end(self):
            self._halo(self.block, [nothing] * len(self.last))

        def _halo(self, block, following):
            here = slice(32 * block, 32 * block + 32)
            prior = self.prior or [nothing] * len(following)
            for lanes, a, b, c in zip(self.halo, prior, self.last, following):
                self.out[here, lanes : lanes + 128] = self.pick(a, b, c)

    def beside(a, b, c):
        return jnp.where(low, c, a)

    def around(a, b, c):
        return jnp.where(low, b, jnp.where(even, c, a))

    volume = Rows(xb1, (0, 128), (256, 384), beside)
    remainder = Rows(xb1, None, (512,), around)
    for w2 in range(20):
        start = 20 - w2
        tiles = []
        for dd in range(2):
            acc = None
            for c in range(8):
                left = jnp.where(low, left_row(c, 2 * w2), left_row(c, 2 * w2 + 1))
                term = left * rs[c, 56 * dd + start : 56 * dd + start + 32]
                acc = term if acc is None else acc + term
            tiles.append(acc * 0.125)
        acc = None
        for c in range(4):
            left = jnp.where(even, left_row(8 + c, 2 * w2), left_row(8 + c, 2 * w2 + 1))
            term = left * rs[8 + c, start : start + 32]
            acc = term if acc is None else acc + term
        rest = (acc + pltpu.roll(acc, 64, axis=1)) * 0.125
        volume.push(w2, [tile.astype(BF) for tile in tiles])
        remainder.push(w2, [rest.astype(BF)])
    volume.end()
    remainder.end()


    class Layer:
        def __init__(self, x, weights, out, cuts):
            own = (0, 128, 512, 640)
            self.rows = Rows(out, own, [lanes + 256 for lanes in own], beside)
            self.x, self.weights = x, weights
            self.chunks = list(zip(cuts, cuts[1:]))

        def step(self):
            first, stop = self.chunks.pop(0)
            y = dot(self.x[32 * first : 32 * stop], self.weights[...])
            for w2 in range(first, stop):
                here = y[32 * (w2 - first) : 32 * (w2 - first) + 32]
                tiles = [
                    here[:, :128] + before(here[:, 256:384]),
                    here[:, 128:256] + after(here[:, 384:]),
                ]
                tiles = [jnp.maximum(tile, 0.0) for tile in tiles]
                if w2 < 2:
                    tiles = [jnp.where(first_ok, tile, 0.0) for tile in tiles]
                if w2 > 17:
                    tiles = [jnp.where(last_ok, tile, 0.0) for tile in tiles]
                high = [tile.astype(BF) for tile in tiles]
                rest = [(tile - part.astype(F32)).astype(BF) for tile, part in zip(tiles, high)]
                self.rows.push(w2, high + rest)
            if not self.chunks:
                self.rows.end()

    layers = [
        Layer(xb1, w1_ref, xb, (0, 7, 14, 20)),
        Layer(xb, wm_ref.at[0], xb2, (1, 6, 13, 19)),
        Layer(xb2, wm_ref.at[1], xb3, (1, 5, 12, 19)),
    ]
    for each in layers:
        for _ in range(len(each.chunks)):
            each.step()
    y = dot(xb3[64:576], wl_ref[...])
    cost = jnp.zeros((32, 128), F32)
    for w2 in range(16):
        part = y[32 * w2 : 32 * w2 + 32]
        part = part if w2 == 0 else pltpu.roll(part, 2 * w2, axis=1)
        cost = jnp.where((lane % 32) // 2 == w2, part, cost)
    moved = jnp.where(low, before(cost), after(cost))
    cost = cost + pltpu.roll(moved, 96, axis=1)
    top = jnp.max(cost, axis=0, keepdims=True)
    top = jnp.maximum(top, pltpu.roll(top, 64, axis=1))
    weight = jnp.exp(cost - top)
    level = (2 * depth + jnp.where(low, 0, 1)).astype(F32) * (1.0 / 64)
    upper = jnp.sum(weight * level, axis=0, keepdims=True)
    under = jnp.sum(weight, axis=0, keepdims=True)
    est = (upper + pltpu.roll(upper, 64, axis=1)) / (under + pltpu.roll(under, 64, axis=1))
    out_ref[...] = est[:, :32]


SCRATCH = [
    pltpu.VMEM((192, 640), BF),
    pltpu.VMEM((12, 112, 128), F32),
    pltpu.VMEM((12, 64, 128), F32),
    pltpu.VMEM((640, 640), BF),
    pltpu.VMEM((640, 1024), BF),
    pltpu.VMEM((640, 1024), BF),
    pltpu.VMEM((640, 1024), BF),
]


def pack_kernel(s_ref, t_ref, own_ref, edge_ref, rights_ref):
    for half, ref in enumerate((s_ref, t_ref)):
        lanes = slice(320 * half, 320 * half + 320)
        right, left = ref[:, :320], ref[:, 320:]
        edge_ref[0:32, lanes] = right
        edge_ref[32:40, lanes] = jnp.concatenate([left[:4], left[28:]], axis=0)
        own_ref[0:32, lanes] = right
        own_ref[32:64, lanes] = left
        rights_ref[:, lanes] = right


def pack(s, t):
    vm = pl.BlockSpec(memory_space=pltpu.VMEM)
    return pl.pallas_call(
        pack_kernel,
        out_shape=[jax.ShapeDtypeStruct((rows, 640), BF) for rows in (64, 40, 32)],
        in_specs=[vm] * 2,
        out_specs=[vm] * 3,
        compiler_params=pltpu.CompilerParams(vmem_limit_bytes=2**20),
        name="pack",
    )(s, t)


def collect_kernel(one_ref, two_ref, s_ref, t_ref, out_ref):
    out_ref[0] = one_ref[...]
    out_ref[1, 0:32] = two_ref[...]
    out_ref[1, 32:40] = jnp.zeros((8, 640), BF)
    for half, ref in enumerate((s_ref, t_ref)):
        lanes = slice(320 * half, 320 * half + 320)
        left = ref[:, 320:]
        out_ref[2, 0:32, lanes] = ref[:, :320]
        out_ref[2, 32:40, lanes] = jnp.concatenate([left[:4], left[28:]], axis=0)


def collect(*parts):
    vm = pl.BlockSpec(memory_space=pltpu.VMEM)
    return pl.pallas_call(
        collect_kernel,
        out_shape=jax.ShapeDtypeStruct((3, 40, 640), BF),
        in_specs=[vm] * 4,
        out_specs=vm,
        compiler_params=pltpu.CompilerParams(vmem_limit_bytes=2**20),
        name="collect",
    )(*parts)


def stage_kernel(s_ref, out_ref):
    out_ref[...] = s_ref[...]


def stage(s):
    vm = pl.BlockSpec(memory_space=pltpu.VMEM)
    return pl.pallas_call(
        stage_kernel,
        out_shape=jax.ShapeDtypeStruct(s.shape, BF),
        in_specs=[vm],
        out_specs=vm,
        compiler_params=pltpu.CompilerParams(vmem_limit_bytes=2**20),
        cost_estimate=pl.CostEstimate(flops=10**9, bytes_accessed=10**6, transcendentals=0),
        name="stage",
    )(s)


def main_kernel(own, other, near, far, w1, wm, wl, perm, out, win, rs, lp, xb1, xb, xb2, xb3):
    z, core = lax.axis_index("disp"), lax.axis_index("cols")
    piece = core * 4 + z

    def load(dp, lo, hi):
        row = jnp.where(iota((hi - lo, 640), 1) < 320, 0, 1)
        if dp == 0:
            return jnp.where(row == 0, own[lo:hi], other[lo:hi])
        want = piece + dp
        ok = (want >= 0) & (want < 8)
        want = jnp.clip(want, 0, 7)
        turn = jnp.maximum((z ^ (want % 4)) - 1, 0)
        flip = core ^ (want // 4)
        part = jnp.where(row == flip, far[turn, lo:hi], near[turn, lo:hi])
        return jnp.where(ok, part, jnp.zeros((), BF))

    def left(dp):
        return load(dp, 32, 64) if dp == 0 else load(dp, 32, 40)

    main_body(load, left, w1, wm, wl, perm, out, win, rs, lp, xb1, xb, xb2, xb3)


def crossed(v, axis, k):
    count = lax.axis_size(axis)
    pairs = [(2 * i + c, 2 * (i ^ k) + 1 - c) for i in range(count) for c in (0, 1)]
    return lax.ppermute(v, (axis, "cols"), pairs)


def fast(left_feat, right_feat, conv_first, conv_mid, conv_last):
    zero = jnp.zeros((), BF)
    s = lax.pad(right_feat[0], zero, ((0, 0, 0), (0, 320, 0))) + lax.pad(
        left_feat[0], zero, ((0, 0, 0), (320, 0, 0))
    )
    t = crossed(s, "rows", 1)
    s_3 = crossed(stage(s), "disp", 3)
    own, edge, rights = pack(s, t)
    swap = [(0, 1), (1, 0)]
    from_1 = crossed(edge, "disp", 1)
    from_2 = crossed(rights, "disp", 2)
    t_3 = crossed(s_3, "rows", 1)
    ws = prep(conv_first, conv_mid, conv_last.reshape(27, 32))
    other = lax.ppermute(own, "cols", swap)
    ws, from_1, from_2, s_3, t_3, other = lax.optimization_barrier(
        (ws, from_1, from_2, s_3, t_3, other)
    )
    near = collect(from_1, from_2, s_3, t_3)
    far = lax.ppermute(near, "cols", swap)
    vm = pl.BlockSpec(memory_space=pltpu.VMEM)
    return pl.pallas_call(
        main_kernel,
        out_shape=jax.ShapeDtypeStruct((1, 32), F32),
        in_specs=[vm] * 8,
        out_specs=vm,
        scratch_shapes=SCRATCH,
        compiler_params=pltpu.CompilerParams(vmem_limit_bytes=24 * 2**20),
        name="cost_volume",
    )(own, other, near, far, *ws)


def shards(left_feat, right_feat, conv_first, conv_mid, conv_last):
    sizes = tuple(lax.axis_size(name) for name in ("disp", "rows", "cols"))
    if sizes == (4, 2, 2) and left_feat.shape == (1, 32, 320) and conv_first.shape == (27, 32, 40):
        return fast(left_feat, right_feat, conv_first, conv_mid, conv_last)
    return general(left_feat, right_feat, conv_first, conv_mid, conv_last)


def solution(mesh):
    return jax.shard_map(
        shards,
        mesh=mesh,
        in_specs=(
            P(("tiles", "rows"), ("cols", "disp"), None),
            P(("tiles", "rows"), ("cols", "disp"), None),
            P(),
            P(),
            P(),
        ),
        out_specs=P(("tiles", "rows"), ("cols", "disp")),
        check_vma=False,
    )
```

```python
import jax
import jax.numpy as jnp
from jax import lax
from jax.experimental import pallas as pl
from jax.experimental.pallas import tpu as pltpu
from jax.sharding import PartitionSpec as P

MID = 2
DDEV = 16


def extended_2(block, sides, width):
    for axis, dim in sides:
        count = lax.axis_size(axis)
        forward = [(i, i + 1) for i in range(count - 1)]
        backward = [(target, source) for source, target in forward]
        low = lax.ppermute(
            lax.slice_in_dim(block, block.shape[dim] - width, None, axis=dim), axis, forward
        )
        high = lax.ppermute(lax.slice_in_dim(block, 0, width, axis=dim), axis, backward)
        block = jnp.concatenate([low, block, high], axis=dim)
    return block


def passed_along(x, axis, by):
    peers = lax.axis_size(axis)
    pairs = [(i, i + by) for i in range(peers) if 0 <= i + by < peers]
    return lax.ppermute(x, axis, pairs)


def combined_all(part, axis, combine):
    gathered = jax.tree.map(lambda a: lax.all_gather(a, axis), part)

    def take(source):
        return jax.tree.map(lambda a: lax.dynamic_index_in_dim(a, source, 0, False), gathered)

    return lax.fori_loop(
        1, lax.axis_size(axis), lambda source, state: combine(state, take(source)), take(0)
    )


def correlate(left_full, extended, groups, first_disp, count, total_disp):
    rows_here, width_here, channels = left_full.shape
    group_size = channels // groups
    left_groups = left_full.reshape(rows_here, width_here, groups, group_size)

    def single(offset):
        disp_value = first_disp + offset
        shifted = lax.dynamic_slice_in_dim(extended, 2 * width_here - disp_value, width_here, 1)
        right_groups = shifted.reshape(rows_here, width_here, groups, group_size)
        corr = (
            jnp.einsum(
                "hwgc,hwgc->ghw", left_groups, right_groups, preferred_element_type=jnp.float32
            )
            / group_size
        )
        inside = (disp_value >= 0) & (disp_value < total_disp)
        return jnp.where(inside, corr, 0.0).astype(jnp.bfloat16)

    return lax.map(single, jnp.arange(count, dtype=jnp.int32))


def convolve(padded, kernel):
    depth_out = padded.shape[0] - 2
    in_chans = padded.shape[1]
    rows_out = padded.shape[2] - 2
    cols_out = padded.shape[3] - 2
    out_chans = kernel.shape[1]
    columns = jnp.concatenate(
        [
            padded[:, :, row_tap : row_tap + rows_out, col_tap : col_tap + cols_out]
            for row_tap in range(3)
            for col_tap in range(3)
        ],
        axis=1,
    )
    flat = columns.reshape(depth_out + 2, 9 * in_chans, rows_out * cols_out)
    summed = jnp.zeros((depth_out, out_chans, rows_out * cols_out), jnp.float32)
    for disp_tap in range(3):
        taps = (
            jnp.transpose(kernel[9 * disp_tap : 9 * disp_tap + 9], (1, 0, 2))
            .reshape(out_chans, 9 * in_chans)
            .astype(flat.dtype)
        )
        summed = summed + jnp.einsum(
            "ok,dkn->don",
            taps,
            flat[disp_tap : disp_tap + depth_out],
            preferred_element_type=jnp.float32,
            precision=lax.Precision.HIGHEST,
        )
    return summed.reshape(depth_out, out_chans, rows_out, cols_out)


def widen(hidden):
    return extended_2(hidden, (("disp", 0), ("rows", 2), ("cols", 3)), 1)


def combine_parts(earlier, later):
    highest = jnp.maximum(earlier[0], later[0])
    scale_one = jnp.exp(earlier[0] - highest)
    scale_two = jnp.exp(later[0] - highest)
    return (
        highest,
        earlier[1] * scale_one + later[1] * scale_two,
        earlier[2] * scale_one + later[2] * scale_two,
    )


def general(left_feat, right_feat, conv_first, conv_mid, conv_last):
    piece_width = left_feat.shape[1]
    groups = conv_first.shape[2]
    disp_count = lax.axis_size("disp")
    depth_here = DDEV
    total_disp = depth_here * disp_count
    first_disp = lax.axis_index("disp") * depth_here
    left_full, right_full = (
        lax.all_gather(left_feat, "disp", axis=1, tiled=True),
        lax.all_gather(right_feat, "disp", axis=1, tiled=True),
    )
    prior_full = passed_along(right_full, "cols", 1)
    extended = jnp.concatenate([jnp.zeros_like(right_full), prior_full, right_full], axis=1)
    volume = correlate(left_full, extended, groups, first_disp, depth_here, total_disp)
    padded = extended_2(volume, (("disp", 0), ("rows", 2), ("cols", 3)), 1)
    hidden = jax.nn.relu(convolve(padded, conv_first))
    for layer in range(MID):
        hidden = jax.nn.relu(convolve(widen(hidden), conv_mid[layer]))
    cost_cube = convolve(widen(hidden), conv_last)[:, 0]
    levels = (
        (first_disp + jnp.arange(depth_here, dtype=jnp.int32)).astype(jnp.float32) / total_disp
    )[:, None, None]
    local_high = jnp.max(cost_cube, axis=0)
    weights = jnp.exp(cost_cube - local_high[None])
    merged = combined_all(
        (local_high, jnp.sum(weights, axis=0), jnp.sum(weights * levels, axis=0)),
        "disp",
        combine_parts,
    )
    whole_row = merged[2] / merged[1]
    return lax.dynamic_slice_in_dim(whole_row, lax.axis_index("disp") * piece_width, piece_width, 1)


BF, F32 = jnp.bfloat16, jnp.float32
NT = (((1,), (1,)), ((), ()))


def dot(a, b, dims=(((1,), (0,)), ((), ()))):
    return lax.dot_general(a, b, dims, preferred_element_type=F32)


def iota(shape, dim):
    return lax.broadcasted_iota(jnp.int32, shape, dim)


def prep_kernel(perm_ref, cf_ref, cm_ref, cl_ref, w1_ref, wm_ref, wl_ref):
    own = lax.axis_index("rows")

    def strip(tap_of, a, h_in, eye):
        rows = []
        for e in (1, 0, -1):
            for h_out in (0, 1):
                rows.append(tap_of(9 * a + 3 * (h_in - h_out + 1) + (e + 1)))
        rows.append(jnp.zeros((64, rows[0].shape[1]), BF))
        return dot(eye, jnp.concatenate(rows, axis=0), NT)

    def halves(base):
        turned = pltpu.roll(base, 64, axis=1)
        found = {1: base[:, :128], -1: base[:, 128:], 2: turned[:, :128], 0: turned[:, 128:]}
        return {w_in: part.astype(BF) for w_in, part in found.items()}

    def fill(ref, at, parts, rows, bases):
        for d_in in (0, 1):
            for w_in in range(-1, 3):
                for base in bases:
                    row = base + at(d_in, w_in)
                    for place, rel in enumerate((0, 1, 2, -1)):
                        a = d_in - rel + 1
                        block = parts[a][w_in] if 0 <= a <= 2 else jnp.zeros((rows, 128), BF)
                        ref[row : row + rows, 128 * place : 128 * place + 128] = block

    def main_row(d_in, w_in):
        return 128 * d_in + {0: 0, 1: 64, 2: 256, -1: 320}[w_in]

    def rest_row(d_in, w_in):
        return 512 + 32 * d_in + {0: 0, 1: 16, 2: 64, -1: 80}[w_in]

    def eye_of(n):
        return (iota((n, n), 0) == iota((n, n), 1)).astype(F32).astype(BF)

    eye40, eye32 = eye_of(40), eye_of(32)
    main, rest = [], []
    for a in range(3):
        parts = [strip(lambda t: cf_ref[t], a, h_in, eye40) for h_in in (0, 1)]
        main.append(halves(jnp.concatenate([p[:32] for p in parts], axis=0)))
        rest.append(halves(jnp.concatenate([p[32:] for p in parts], axis=0)))
    fill(w1_ref, main_row, main, 64, (0,))
    fill(w1_ref, rest_row, rest, 16, (0,))
    for layer in range(2):
        main = [
            halves(
                jnp.concatenate(
                    [strip(lambda t: cm_ref[layer, t], a, h_in, eye32) for h_in in (0, 1)], axis=0
                )
            )
            for a in range(3)
        ]
        fill(wm_ref.at[layer], main_row, main, 64, (0, 512))
    clt = dot(eye32, cl_ref[...], NT).astype(BF)
    lane = iota((27, 128), 1)
    rel = jnp.where(lane < 32, 0, jnp.where(lane < 64, 2, jnp.where(lane < 96, 1, -1)))
    for d_in in (0, 1):
        for w_in in range(-1, 3):
            for h_in in (0, 1):
                a, e, b = d_in - rel, w_in - lane % 32, h_in - own
                tap = 9 * (a + 1) + 3 * (b + 1) + (e + 1)
                ok = (lane % 32 < 2) & (a >= -1) & (a <= 1) & (e >= -1) & (e <= 1) & (b >= -1) & (b <= 1)
                pick = (ok & (iota((27, 128), 0) == tap)).astype(F32).astype(BF)
                block = dot(clt, pick).astype(BF)
                row = main_row(d_in, w_in) + 32 * h_in
                wl_ref[row : row + 32] = block
                wl_ref[512 + row : 544 + row] = block


def perm_kernel(perm_ref):
    own = lax.axis_index("rows")
    lane = iota((1, 512), 1)
    src = (((lane // 32) % 2) ^ own) * 320 + (lane % 32) * 8 + lane // 64
    perm_ref[:, :512] = (iota((640, 512), 0) == src).astype(F32).astype(BF)
    lane = iota((1, 512), 1)
    src = (((lane // 8) % 2) ^ own) * 320 + (32 + lane % 8) * 8 + (lane // 128) * 2 + (lane // 64) % 2
    perm_ref[:, 512:] = (iota((640, 512), 0) == src).astype(F32).astype(BF)


def prep(cf, cm, cl):
    vm = pl.BlockSpec(memory_space=pltpu.VMEM)
    perm = pl.pallas_call(
        perm_kernel,
        out_shape=jax.ShapeDtypeStruct((640, 1024), BF),
        out_specs=vm,
        compiler_params=pltpu.CompilerParams(vmem_limit_bytes=8 * 2**20),
        cost_estimate=pl.CostEstimate(flops=10**9, bytes_accessed=3 * 10**6, transcendentals=0),
        name="perm",
    )()
    ws = pl.pallas_call(
        prep_kernel,
        out_shape=(
            jax.ShapeDtypeStruct((640, 512), BF),
            jax.ShapeDtypeStruct((2, 1024, 512), BF),
            jax.ShapeDtypeStruct((1024, 128), BF),
        ),
        in_specs=[vm] * 4,
        out_specs=[vm] * 3,
        compiler_params=pltpu.CompilerParams(vmem_limit_bytes=16 * 2**20),
        cost_estimate=pl.CostEstimate(flops=2 * 10**9, bytes_accessed=4 * 10**6, transcendentals=0),
        name="prep",
    )(perm, cf, cm, cl)
    return (*ws, perm)


def main_body(load_r, load_l, w1_ref, wm_ref, wl_ref, perm_ref, out_ref, win, rs, lp, xb1, xb, xb2, xb3):
    z = lax.axis_index("disp")
    core = lax.axis_index("cols")
    piece = core * 4 + z
    win[...] = jnp.zeros_like(win)

    def put(row, part):
        win[row : row + part.shape[0]] = part

    put(0, load_r(1, 0, 16))
    put(16, load_r(-3, 16, 32))
    put(32, load_r(-2, 0, 32))
    put(64, load_r(-1, 0, 32))
    put(96, load_r(0, 0, 32))
    put(136, load_l(-1))
    put(144, load_l(0))
    put(176, load_l(1))
    zp = dot(win[...], perm_ref[...])
    halfway = iota((128, 128), 1) < 64
    near_half, far_half = [], []
    for tile in range(4):
        straight = zp[:, 128 * tile : 128 * tile + 128]
        turned = pltpu.roll(straight, 64, axis=1)
        for even, a, b in ((0, straight, turned), (1, turned, straight)):
            near_half.append(jnp.where(halfway, a[:128], 0.0).astype(BF))
            far_half.append(jnp.where(halfway, 0.0, b[:128]).astype(BF))
            lp[2 * tile + even] = jnp.where(halfway[:64], a[128:], pltpu.roll(b[128:], 63, axis=0))
    for tile in range(4):
        this = zp[128:, 512 + 128 * tile : 640 + 128 * tile]
        first = (iota((64, 128), 1) // 16) % 2 == 0
        lp[8 + tile] = jnp.where(first, this, pltpu.roll(this, 63, axis=0))
    zm = jnp.concatenate(
        [jnp.concatenate(near_half, axis=1), jnp.concatenate(far_half, axis=1)], axis=0
    )
    zpr = zp[:128]
    lane = iota((128, 512), 1)
    ze = jnp.concatenate(
        [jnp.where((lane // 16) % 4 == ww, zpr[:, 512:], 0.0).astype(BF) for ww in range(4)], axis=0
    )
    s, q = iota((112, 256), 0), iota((112, 256), 1)
    r = q % 128
    rel = jnp.where(r < 16, 32 + r, r - 96)
    dd = jnp.where(s < 56, 0, 1)
    pick = (rel == 36 + q // 128 - dd - 2 * (s - 56 * dd)).astype(F32).astype(BF)
    rsm = dot(pick, zm)
    s, q = iota((56, 512), 0), iota((56, 512), 1)
    r = q % 128
    rel = jnp.where(r < 16, 32 + r, r - 96)
    pick = (rel == 36 + (q // 128) % 2 - q // 256 - 2 * s).astype(F32).astype(BF)
    rse = dot(pick, ze)
    for tile in range(8):
        rs[tile] = rsm[:, 128 * tile : 128 * tile + 128]
    for tile in range(4):
        rs[8 + tile, 0:56] = rse[:, 128 * tile : 128 * tile + 128]

    lane = iota((32, 128), 1)
    low, even = lane < 64, (lane // 16) % 2 == 0
    depth = iota((32, 128), 0)
    nothing = jnp.zeros((32, 128), BF)
    first_ok = piece > 0
    last_ok = piece < 4 * lax.axis_size("cols") - 1

    def before(tile):
        return jnp.where(depth == 0, 0.0, pltpu.roll(tile, 1, axis=0))

    def after(tile):
        return jnp.where(depth == 31, 0.0, pltpu.roll(tile, 31, axis=0))

    class Rows:
        def __init__(self, out, own_lanes, halo_lanes, pick):
            self.out, self.own, self.halo, self.pick = out, own_lanes, halo_lanes, pick
            self.last, self.prior = None, None

        def push(self, block, values):
            if self.last is not None:
                self._halo(block - 1, values)
            here = slice(32 * block, 32 * block + 32)
            if self.own is not None:
                for lanes, value in zip(self.own, values):
                    self.out[here, lanes : lanes + 128] = value
            self.prior, self.last = self.last, values
            self.block = block

        def end(self):
            self._halo(self.block, [nothing] * len(self.last))

        def _halo(self, block, following):
            here = slice(32 * block, 32 * block + 32)
            prior = self.prior or [nothing] * len(following)
            for lanes, a, b, c in zip(self.halo, prior, self.last, following):
                self.out[here, lanes : lanes + 128] = self.pick(a, b, c)

    def beside(a, b, c):
        return jnp.where(low, c, a)

    def around(a, b, c):
        return jnp.where(low, b, jnp.where(even, c, a))

    def spread(block, value, own_lanes, halo_lanes):
        xb1[32 * block : 32 * block + 32, own_lanes : own_lanes + 128] = value
        if block > 0:
            xb1[32 * block - 32 : 32 * block, halo_lanes : halo_lanes + 64] = value[:, :64]
        if block < 19:
            xb1[32 * block + 32 : 32 * block + 64, halo_lanes + 64 : halo_lanes + 128] = value[:, 64:]

    for halo in (256, 384):
        xb1[0:32, halo + 64 : halo + 128] = nothing[:, :64]
        xb1[608:640, halo : halo + 64] = nothing[:, :64]
    rests = {}
    for phase in range(8):
        group = range(phase, 20, 8)
        base = 20 - group[-1]
        count = 24 + 8 * len(group)
        ats = [8 * (len(group) - 1 - index) for index in range(len(group))]
        sums = [[None, None, None] for _ in group]
        for c in range(12):
            for dd in range(2 if c < 8 else 1):
                right = rs[c, 56 * dd + base : 56 * dd + base + count]
                for w2, at, acc in zip(group, ats, sums):
                    left = lp[c, 12 + 2 * w2 : 13 + 2 * w2]
                    term = left * right[at : at + 32]
                    which = dd if c < 8 else 2
                    acc[which] = term if acc[which] is None else acc[which] + term
        for w2, acc in zip(group, sums):
            spread(w2, (acc[0] * 0.125).astype(BF), 0, 256)
            spread(w2, (acc[1] * 0.125).astype(BF), 128, 384)
            rests[w2] = ((acc[2] + pltpu.roll(acc[2], 64, axis=1)) * 0.125).astype(BF)
    remainder = Rows(xb1, None, (512,), around)
    for w2 in range(20):
        remainder.push(w2, [rests[w2]])
    remainder.end()

    class Layer:
        def __init__(self, x, weights, out, cuts):
            own = (0, 128, 512, 640)
            self.rows = Rows(out, own, [lanes + 256 for lanes in own], beside)
            self.x, self.weights = x, weights
            self.chunks = list(zip(cuts, cuts[1:]))

        def step(self):
            first, stop = self.chunks.pop(0)
            y = dot(self.x[32 * first : 32 * stop], self.weights[...])
            for w2 in range(first, stop):
                here = y[32 * (w2 - first) : 32 * (w2 - first) + 32]
                tiles = [
                    here[:, :128] + before(here[:, 256:384]),
                    here[:, 128:256] + after(here[:, 384:]),
                ]
                tiles = [jnp.maximum(tile, 0.0) for tile in tiles]
                if w2 < 2:
                    tiles = [jnp.where(first_ok, tile, 0.0) for tile in tiles]
                if w2 > 17:
                    tiles = [jnp.where(last_ok, tile, 0.0) for tile in tiles]
                high = [tile.astype(BF) for tile in tiles]
                rest = [(tile - part.astype(F32)).astype(BF) for tile, part in zip(tiles, high)]
                self.rows.push(w2, high + rest)
            if not self.chunks:
                self.rows.end()

    layers = [
        Layer(xb1, w1_ref, xb, (0, 7, 14, 20)),
        Layer(xb, wm_ref.at[0], xb2, (1, 6, 13, 19)),
        Layer(xb2, wm_ref.at[1], xb3, (1, 5, 12, 19)),
    ]
    for each in layers:
        for _ in range(len(each.chunks)):
            each.step()
    y = dot(xb3[64:576], wl_ref[...])
    cost = jnp.zeros((32, 128), F32)
    for w2 in range(16):
        part = y[32 * w2 : 32 * w2 + 32]
        part = part if w2 == 0 else pltpu.roll(part, 2 * w2, axis=1)
        cost = jnp.where((lane % 32) // 2 == w2, part, cost)
    moved = jnp.where(low, before(cost), after(cost))
    cost = cost + pltpu.roll(moved, 96, axis=1)
    top = jnp.max(cost, axis=0, keepdims=True)
    top = jnp.maximum(top, pltpu.roll(top, 64, axis=1))
    weight = jnp.exp(cost - top)
    level = (2 * depth + jnp.where(low, 0, 1)).astype(F32) * (1.0 / 64)
    upper = jnp.sum(weight * level, axis=0, keepdims=True)
    under = jnp.sum(weight, axis=0, keepdims=True)
    est = (upper + pltpu.roll(upper, 64, axis=1)) / (under + pltpu.roll(under, 64, axis=1))
    out_ref[...] = est[:, :32]


SCRATCH = [
    pltpu.VMEM((192, 640), BF),
    pltpu.VMEM((12, 112, 128), F32),
    pltpu.VMEM((12, 64, 128), F32),
    pltpu.VMEM((640, 640), BF),
    pltpu.VMEM((640, 1024), BF),
    pltpu.VMEM((640, 1024), BF),
    pltpu.VMEM((640, 1024), BF),
]


def pack_kernel(s_ref, t_ref, own_ref, edge_ref, rights_ref):
    for half, ref in enumerate((s_ref, t_ref)):
        lanes = slice(320 * half, 320 * half + 320)
        right, left = ref[:, :320], ref[:, 320:]
        edge_ref[0:32, lanes] = right
        edge_ref[32:40, lanes] = jnp.concatenate([left[:4], left[28:]], axis=0)
        own_ref[0:32, lanes] = right
        own_ref[32:64, lanes] = left
        rights_ref[:, lanes] = right


def pack(s, t):
    vm = pl.BlockSpec(memory_space=pltpu.VMEM)
    return pl.pallas_call(
        pack_kernel,
        out_shape=[jax.ShapeDtypeStruct((rows, 640), BF) for rows in (64, 40, 32)],
        in_specs=[vm] * 2,
        out_specs=[vm] * 3,
        compiler_params=pltpu.CompilerParams(vmem_limit_bytes=2**20),
        name="pack",
    )(s, t)


def collect_kernel(one_ref, two_ref, s_ref, t_ref, out_ref):
    out_ref[0] = one_ref[...]
    out_ref[1, 0:32] = two_ref[...]
    out_ref[1, 32:40] = jnp.zeros((8, 640), BF)
    for half, ref in enumerate((s_ref, t_ref)):
        lanes = slice(320 * half, 320 * half + 320)
        left = ref[:, 320:]
        out_ref[2, 0:32, lanes] = ref[:, :320]
        out_ref[2, 32:40, lanes] = jnp.concatenate([left[:4], left[28:]], axis=0)


def collect(*parts):
    vm = pl.BlockSpec(memory_space=pltpu.VMEM)
    return pl.pallas_call(
        collect_kernel,
        out_shape=jax.ShapeDtypeStruct((3, 40, 640), BF),
        in_specs=[vm] * 4,
        out_specs=vm,
        compiler_params=pltpu.CompilerParams(vmem_limit_bytes=2**20),
        name="collect",
    )(*parts)


def stage_kernel(s_ref, out_ref):
    out_ref[...] = s_ref[...]


def stage(s):
    vm = pl.BlockSpec(memory_space=pltpu.VMEM)
    return pl.pallas_call(
        stage_kernel,
        out_shape=jax.ShapeDtypeStruct(s.shape, BF),
        in_specs=[vm],
        out_specs=vm,
        compiler_params=pltpu.CompilerParams(vmem_limit_bytes=2**20),
        cost_estimate=pl.CostEstimate(flops=10**9, bytes_accessed=10**6, transcendentals=0),
        name="stage",
    )(s)


def main_kernel(own, other, near, far, w1, wm, wl, perm, out, win, rs, lp, xb1, xb, xb2, xb3):
    z, core = lax.axis_index("disp"), lax.axis_index("cols")
    piece = core * 4 + z

    def load(dp, lo, hi):
        row = jnp.where(iota((hi - lo, 640), 1) < 320, 0, 1)
        if dp == 0:
            return jnp.where(row == 0, own[lo:hi], other[lo:hi])
        want = piece + dp
        ok = (want >= 0) & (want < 8)
        want = jnp.clip(want, 0, 7)
        turn = jnp.maximum((z ^ (want % 4)) - 1, 0)
        flip = core ^ (want // 4)
        part = jnp.where(row == flip, far[turn, lo:hi], near[turn, lo:hi])
        return jnp.where(ok, part, jnp.zeros((), BF))

    def left(dp):
        return load(dp, 32, 64) if dp == 0 else load(dp, 32, 40)

    main_body(load, left, w1, wm, wl, perm, out, win, rs, lp, xb1, xb, xb2, xb3)


def crossed(v, axis, k):
    count = lax.axis_size(axis)
    pairs = [(2 * i + c, 2 * (i ^ k) + 1 - c) for i in range(count) for c in (0, 1)]
    return lax.ppermute(v, (axis, "cols"), pairs)


def fast(left_feat, right_feat, conv_first, conv_mid, conv_last):
    zero = jnp.zeros((), BF)
    s = lax.pad(right_feat[0], zero, ((0, 0, 0), (0, 320, 0))) + lax.pad(
        left_feat[0], zero, ((0, 0, 0), (320, 0, 0))
    )
    t = crossed(s, "rows", 1)
    s_3 = crossed(stage(s), "disp", 3)
    own, edge, rights = pack(s, t)
    swap = [(0, 1), (1, 0)]
    from_1 = crossed(edge, "disp", 1)
    from_2 = crossed(rights, "disp", 2)
    t_3 = crossed(s_3, "rows", 1)
    ws = prep(conv_first, conv_mid, conv_last.reshape(27, 32))
    other = lax.ppermute(own, "cols", swap)
    ws, from_1, from_2, s_3, t_3, other = lax.optimization_barrier(
        (ws, from_1, from_2, s_3, t_3, other)
    )
    near = collect(from_1, from_2, s_3, t_3)
    far = lax.ppermute(near, "cols", swap)
    vm = pl.BlockSpec(memory_space=pltpu.VMEM)
    return pl.pallas_call(
        main_kernel,
        out_shape=jax.ShapeDtypeStruct((1, 32), F32),
        in_specs=[vm] * 8,
        out_specs=vm,
        scratch_shapes=SCRATCH,
        compiler_params=pltpu.CompilerParams(vmem_limit_bytes=24 * 2**20),
        name="cost_volume",
    )(own, other, near, far, *ws)


def shards(left_feat, right_feat, conv_first, conv_mid, conv_last):
    sizes = tuple(lax.axis_size(name) for name in ("disp", "rows", "cols"))
    if sizes == (4, 2, 2) and left_feat.shape == (1, 32, 320) and conv_first.shape == (27, 32, 40):
        return fast(left_feat, right_feat, conv_first, conv_mid, conv_last)
    return general(left_feat, right_feat, conv_first, conv_mid, conv_last)


def solution(mesh):
    return jax.shard_map(
        shards,
        mesh=mesh,
        in_specs=(
            P(("tiles", "rows"), ("cols", "disp"), None),
            P(("tiles", "rows"), ("cols", "disp"), None),
            P(),
            P(),
            P(),
        ),
        out_specs=P(("tiles", "rows"), ("cols", "disp")),
        check_vma=False,
    )
```
